256 devices in a mesh: gx: 8 (over y, core), gy: 4 (over x), gz: 8 (over z).
Axes of the slice: x: 4, y: 4, z: 8, core: 2. Of those that a mesh axis runs over, the one named last changes fastest.
Arguments:
- phase_stack: float32 [512, 524288], P(None, ('gx', 'gy', 'gz')), may hold values from -40 to 40
- start_basis: float32 [512, 64], replicated, may hold values from -6 to 6
Outputs:
- corrected: float32 [512, 524288], P(None, ('gx', 'gy', 'gz'))
The draws below stay inside these ranges and needn't reach their ends.
All inputs are finite; a program needn't handle non-finite values.
Results may differ from the reference program's by a relative error of at most 0.0003.
Values sent between devices are 32-bit elements; how exact they have to be, the bound alone decides.
No kernel may reach another device: no remote copies, remote signals or barrier semaphores. Data moves between devices by JAX's collectives and lax.ppermute only.
A program may use at most 64 MiB of HBM per device.

```python
import math
import jax
import jax.numpy as jnp
from jax import lax

M = 512
K = 64
ITERS = 3
NPIX = 524288


def draw_phase_stack(key, part):
    base = jax.random.fold_in(key, 11)
    key_mix = jax.random.fold_in(base, 0)
    key_amp = jax.random.fold_in(base, 1)
    key_src = jax.random.fold_in(base, 2)
    key_clutter = jax.random.fold_in(base, 4)
    mixing = jax.random.normal(key_mix, (M, K), jnp.float32) / math.sqrt(M)
    amplitude = jnp.exp(jax.random.uniform(key_amp, (K,), jnp.float32, 0.0, math.log(4.2)))
    sources = jax.random.normal(key_src, (K, NPIX), jnp.float32)
    position = jnp.arange(NPIX, dtype=jnp.float32) / NPIX
    clutter_scale = 1.0 + 2.0 * position
    clutter = jax.random.normal(key_clutter, (M, NPIX), jnp.float32)
    signal = jnp.dot(mixing * amplitude[None, :], sources, precision=lax.Precision.HIGHEST)
    return jnp.clip(signal + clutter * clutter_scale[None, :], -40.0, 40.0)


def centred(key, shape, spread, most, kind=jnp.bfloat16):
    array = spread * jax.random.normal(key, shape, jnp.float32)
    return jnp.clip(array, min=-most, max=most).astype(kind)


def setup_inputs(seed: int = 0) -> dict:
    splits = jax.random.split(jax.random.key(seed), 3)
    return {
        "phase_stack": draw_phase_stack(jax.random.fold_in(splits[2], 71), 0),
        "start_basis": centred(splits[1], (M, K), 1.0, 6.0, jnp.float32),
    }


HIGHEST = lax.Precision.HIGHEST
EPSILON = 1e-06

def orthonormal(columns):
    inner_gram = jnp.dot(columns.T, columns, precision=HIGHEST)
    cholesky_factor = jnp.linalg.cholesky(inner_gram)
    return jax.scipy.linalg.solve_triangular(cholesky_factor, columns.T, lower=True).T

def reference(phase_stack, start_basis):
    pixel_total = phase_stack.shape[1]
    gram_matrix = jnp.dot(phase_stack, phase_stack.T, precision=HIGHEST) / pixel_total
    subspace = orthonormal(start_basis)
    for sweep in range(ITERS):
        subspace = orthonormal(jnp.dot(gram_matrix, subspace, precision=HIGHEST))
    loadings = jnp.dot(subspace.T, phase_stack, precision=HIGHEST)
    residual = phase_stack - jnp.dot(subspace, loadings, precision=HIGHEST)
    row_power = lax.optimization_barrier(jnp.sum(residual * residual, axis=1)) / pixel_total
    return residual * lax.rsqrt(row_power + EPSILON)[:, None]
```

```python
import jax
import jax.numpy as jnp
from jax import lax
from jax.sharding import Mesh
from jax.sharding import PartitionSpec as P

ITERS = 3
AXES = ("y", "c", "x", "z")
HIGH = lax.Precision.HIGH
HIGHEST = lax.Precision.HIGHEST
EPSILON = 1e-06
TILE = 128


def shifted(v, axis, step):
    n = lax.axis_size(axis)
    return lax.ppermute(v, axis, [(i, (i + step) % n) for i in range(n)])


def share_of_sum(v, axis):
    n, me = lax.axis_size(axis), lax.axis_index(axis)
    rows = v.shape[0] // n
    piece = lambda k: lax.dynamic_slice_in_dim(v, lax.rem(me + k, n) * rows, rows, 0)
    arrived = [shifted(piece(k), axis, k) for k in range(1, n)]
    total = piece(0)
    for part in arrived:
        total = total + part
    return total


def joined(v, axis):
    n, me = lax.axis_size(axis), lax.axis_index(axis)
    rows = v.shape[0]
    arrived = [shifted(v, axis, k) for k in range(1, n)]
    whole = jnp.zeros((n * rows, *v.shape[1:]), v.dtype)
    whole = lax.dynamic_update_slice_in_dim(whole, v, me * rows, 0)
    for k, part in enumerate(arrived, 1):
        whole = lax.dynamic_update_slice_in_dim(whole, part, lax.rem(me - k + n, n) * rows, 0)
    return whole


def summed(v, axis):
    n = lax.axis_size(axis)
    copies = jnp.broadcast_to(v[None], (n, *v.shape)).reshape(n * v.shape[0], *v.shape[1:])
    arrived = lax.all_to_all(copies, axis, 0, 0, tiled=True)
    return arrived.reshape(n, *v.shape).sum(axis=0)


def sum_everywhere(v):
    v = share_of_sum(v, "c")
    v = share_of_sum(v, "y")
    v = share_of_sum(v, "x")
    v = summed(v, "z")
    v = joined(v, "x")
    v = joined(v, "y")
    return joined(v, "c")


def packed(gram):
    n = gram.shape[0] // TILE
    tiles = gram.reshape(n, TILE, n, TILE)
    return jnp.concatenate([tiles[i, :, j] for i in range(n) for j in range(i, n)], axis=0)


def unpacked(lines, n):
    tiles = {}
    place = 0
    for i in range(n):
        for j in range(i, n):
            tile = lines[place * TILE : (place + 1) * TILE]
            tiles[i, j] = tile
            tiles[j, i] = tile.T
            place += 1
    return jnp.block([[tiles[i, j] for j in range(n)] for i in range(n)])


def orthonormal(columns):
    inner_gram = jnp.dot(columns.T, columns, precision=HIGHEST)
    cholesky_factor = jnp.linalg.cholesky(inner_gram)
    return jax.scipy.linalg.solve_triangular(cholesky_factor, columns.T, lower=True).T


def on_device(phase_stack, start_basis):
    pixel_total = phase_stack.shape[1] * lax.axis_size(AXES)
    subspace = orthonormal(start_basis)
    local_gram = jnp.dot(phase_stack, phase_stack.T, precision=HIGHEST)
    lines = sum_everywhere(packed(local_gram))
    gram_matrix = unpacked(lines, local_gram.shape[0] // TILE) / pixel_total
    for sweep in range(ITERS):
        subspace = orthonormal(jnp.dot(gram_matrix, subspace, precision=HIGHEST))
    left = gram_matrix - jnp.dot(
        subspace, jnp.dot(subspace.T, gram_matrix, precision=HIGHEST), precision=HIGHEST
    )
    across = jnp.dot(left, subspace, precision=HIGHEST)
    row_power = jnp.diagonal(left) - jnp.sum(across * subspace, axis=1)
    row_scale = lax.rsqrt(jnp.maximum(row_power, 0.0) + EPSILON)[:, None]
    loadings = jnp.dot(subspace.T, phase_stack, precision=HIGH)
    return (phase_stack - jnp.dot(subspace, loadings, precision=HIGH)) * row_scale


def solution(mesh):
    split = Mesh(mesh.devices.reshape(-1, 2, mesh.shape["gy"], mesh.shape["gz"]), AXES)
    placed = (P(None, AXES), P())
    return jax.shard_map(
        on_device, mesh=split, in_specs=placed, out_specs=P(None, AXES), check_vma=False
    )
```

```python
import functools

import jax
import jax.numpy as jnp
from jax import lax
from jax.experimental import pallas as pl
from jax.experimental.pallas import tpu as pltpu
from jax.sharding import Mesh
from jax.sharding import PartitionSpec as P

ITERS = 3
AXES = ("y", "c", "x", "z")
HIGHEST = lax.Precision.HIGHEST
EPSILON = 1e-06
TILE = 128
WIDE = 256
ROWS = 8
F32 = jnp.float32
BF16 = jnp.bfloat16
NT = (((1,), (1,)), ((), ()))


def partner(v, axis, k):
    return lax.ppermute(v, axis, [(i, i ^ k) for i in range(lax.axis_size(axis))])


def share_of_sum(v, axis):
    n, me = lax.axis_size(axis), lax.axis_index(axis)
    rows = v.shape[0] // n
    piece = lambda k: lax.dynamic_slice_in_dim(v, (me ^ k) * rows, rows, 0)
    arrived = [partner(piece(k), axis, k) for k in range(1, n)]
    total = piece(0)
    for part in arrived:
        total = total + part
    return total


def joined(v, axis):
    return jnp.concatenate([v] + [partner(v, axis, k) for k in range(1, lax.axis_size(axis))], axis=0)


def summed(v, axis):
    n = lax.axis_size(axis)
    copies = jnp.broadcast_to(v[None], (n, *v.shape)).reshape(n * v.shape[0], *v.shape[1:])
    arrived = lax.all_to_all(copies, axis, 0, 0, tiled=True)
    return arrived.reshape(n, *v.shape).sum(axis=0)


def sum_everywhere(v):
    v = share_of_sum(v, "c")
    v = share_of_sum(v, "y")
    v = share_of_sum(v, "x")
    v = summed(v, "z")
    v = joined(v, "x")
    v = joined(v, "y")
    return joined(v, "c")


def two_parts(x):
    hi = x.astype(BF16)
    return hi, (x - hi.astype(F32)).astype(BF16)


def three_parts(x):
    hi = x.astype(BF16)
    rest = x - hi.astype(F32)
    mid = rest.astype(BF16)
    return hi, mid, (rest - mid.astype(F32)).astype(BF16)


def dot(a, b):
    return jnp.dot(a, b, preferred_element_type=F32)


def dot_nt(a, b, precision=None):
    return lax.dot_general(a, b, NT, precision=precision, preferred_element_type=F32)


def iota(shape, dim):
    return lax.broadcasted_iota(jnp.int32, shape, dim)


def gram_kernel(x_ref, out_ref, total):
    step = pl.program_id(0)
    m = x_ref.shape[0]

    @pl.when(step == 0)
    def _():
        total[...] = jnp.zeros_like(total)

    hi, lo = two_parts(x_ref[...])
    for j in range(m // WIDE):
        rows, here = slice(0, (j + 1) * WIDE), slice(j * WIDE, (j + 1) * WIDE)
        total[rows, here] += (
            dot_nt(hi[rows], hi[here]) + dot_nt(lo[rows], hi[here]) + dot_nt(hi[rows], lo[here])
        )

    @pl.when(step == pl.num_programs(0) - 1)
    def _():
        place = 0
        for i in range(m // TILE):
            for j in range(i, m // TILE):
                out_ref[place * TILE : (place + 1) * TILE, :] = total[
                    i * TILE : (i + 1) * TILE, j * TILE : (j + 1) * TILE
                ]
                place += 1


def upper_gram(x, chunk=512):
    m, n = x.shape
    tiles = m // TILE
    lines = tiles * (tiles + 1) // 2 * TILE
    return pl.pallas_call(
        gram_kernel,
        out_shape=jax.ShapeDtypeStruct((lines, TILE), F32),
        grid=(n // chunk,),
        in_specs=[pl.BlockSpec((m, chunk), lambda i: (0, i))],
        out_specs=pl.BlockSpec((lines, TILE), lambda i: (0, 0)),
        scratch_shapes=[pltpu.VMEM((m, m), F32)],
        compiler_params=pltpu.CompilerParams(vmem_limit_bytes=32 * 2**20),
        cost_estimate=pl.CostEstimate(flops=6 * m * m * n, bytes_accessed=4 * m * n, transcendentals=0),
        name="gram",
    )(x)


def inverse_factor(b):
    k = b.shape[0]
    blocks = k // ROWS
    eye = (iota((k, k), 0) == iota((k, k), 1)).astype(F32)
    both = jnp.concatenate([b, eye], axis=1)
    line = [both[ROWS * q : ROWS * (q + 1), :] for q in range(blocks)]
    sub = iota((ROWS, 2 * k), 0)
    for p in range(blocks):
        column = {
            (q, i): jnp.broadcast_to(line[q][:, ROWS * p + i : ROWS * p + i + 1], (ROWS, 2 * k))
            for q in range(p, blocks)
            for i in range(ROWS)
        }
        for i in range(ROWS):
            inverse = 1.0 / column[p, i][i : i + 1, :]
            pivot_row = line[p][i : i + 1, :] * inverse
            ahead = {j: column[p, j][i : i + 1, :] * inverse for j in range(i + 1, ROWS)}
            for q in range(p, blocks):
                factor = column[q, i]
                if q == p:
                    factor = jnp.where(sub > i, factor, 0.0)
                for j in range(i + 1, ROWS):
                    column[q, j] = column[q, j] - factor * ahead[j]
                line[q] = line[q] - factor * pivot_row
    both = jnp.concatenate(line, axis=0)
    pivots = jnp.sum(
        jnp.where(iota(both.shape, 0) == iota(both.shape, 1), both, 0.0), axis=1, keepdims=True
    )
    return (both * lax.rsqrt(pivots))[:, k:]


def orthonormal(y):
    return jnp.dot(inverse_factor(dot_nt(y, y, HIGHEST)), y, precision=HIGHEST)


def start_kernel(s_ref, v_ref):
    v_ref[...] = orthonormal(s_ref[...].T)


def start_rows(s):
    m, k = s.shape
    return pl.pallas_call(
        start_kernel,
        out_shape=jax.ShapeDtypeStruct((k, m), F32),
        cost_estimate=pl.CostEstimate(flops=8 * 10**9, bytes_accessed=8 * m * k, transcendentals=0),
        name="start_rows",
    )(s)


def times_gram(v, gram):
    k = v.shape[0]
    v0, v1, v2 = three_parts(v)
    first = dot(jnp.concatenate([v0, v1, v2], axis=0), gram[0][...])
    second = dot(jnp.concatenate([v0, v1], axis=0), gram[1][...])
    third = dot(v0, gram[2][...])
    return first[:k] + (
        (first[k : 2 * k] + second[:k]) + ((first[2 * k :] + second[k:]) + third)
    )


def finish_kernel(pixel_total, chunk, me_ref, lines_ref, v_ref, x_hbm, out_hbm, x, out, ordered, g0, g1, g2, x_sem, out_sem):
    m, n = x_hbm.shape
    k = v_ref.shape[0]
    tiles = m // TILE
    load = pltpu.make_async_copy(x_hbm, x, x_sem)
    load.start()
    slots = 32
    rows = lines_ref.shape[0] // slots
    me = me_ref[0]
    for slot in range(slots):
        place = pl.multiple_of((me ^ slot) * rows, ROWS)
        ordered[pl.ds(place, rows), :] = lines_ref[slot * rows : (slot + 1) * rows, :]

    gram = (g0, g1, g2)
    diagonal = []
    place = 0
    for i in range(tiles):
        for j in range(i, tiles):
            tile = ordered[place * TILE : (place + 1) * TILE, :] * (1.0 / pixel_total)
            place += 1
            at_i, at_j = slice(i * TILE, (i + 1) * TILE), slice(j * TILE, (j + 1) * TILE)
            for ref, part in zip(gram, three_parts(tile)):
                ref[at_i, at_j] = part
            if i == j:
                eye = iota((TILE, TILE), 0) == iota((TILE, TILE), 1)
                diagonal.append(jnp.sum(jnp.where(eye, tile, 0.0), axis=0, keepdims=True))
            else:
                for ref, part in zip(gram, three_parts(tile.T)):
                    ref[at_j, at_i] = part

    v = v_ref[...]
    for sweep in range(ITERS):
        v = orthonormal(times_gram(v, gram))
    w = times_gram(v, gram)
    inner = dot_nt(w, v, HIGHEST)
    twice = jnp.dot(inner, v, precision=HIGHEST) - 2.0 * w
    power = jnp.concatenate(diagonal, axis=1) + jnp.sum(v * twice, axis=0, keepdims=True)
    scale = lax.rsqrt(jnp.maximum(power, 0.0) + EPSILON)
    scale = jnp.concatenate(
        [
            jnp.broadcast_to(scale[:, i * TILE : (i + 1) * TILE], (TILE, TILE)).T
            for i in range(tiles)
        ],
        axis=0,
    )
    q0, q1 = two_parts(v.T)
    spread = jnp.concatenate([q0, q1, q0], axis=1)
    v0, v1 = two_parts(v)
    v01 = jnp.concatenate([v0, v1], axis=0)
    load.wait()
    for c in range(n // chunk):
        here = slice(c * chunk, (c + 1) * chunk)
        xc = x[:, here]
        x0, x1 = two_parts(xc)
        both = dot(v01, x0)
        l0, l1 = two_parts(both[:k] + (both[k:] + dot(v0, x1)))
        common = dot(spread, jnp.concatenate([l0, l0, l1], axis=0))
        for t in range(chunk // TILE):
            at = slice(t * TILE, (t + 1) * TILE)
            out[:, c * chunk + t * TILE : c * chunk + (t + 1) * TILE] = (xc[:, at] - common[:, at]) * scale
        pltpu.make_async_copy(out.at[:, here], out_hbm.at[:, here], out_sem.at[c]).start()
    for c in range(n // chunk):
        here = slice(c * chunk, (c + 1) * chunk)
        pltpu.make_async_copy(out.at[:, here], out_hbm.at[:, here], out_sem.at[c]).wait()


def corrected(lines, me, v, x, pixel_total, chunk=512):
    m, n = x.shape
    k = v.shape[0]
    return pl.pallas_call(
        functools.partial(finish_kernel, pixel_total, chunk),
        out_shape=jax.ShapeDtypeStruct((m, n), F32),
        in_specs=[
            pl.BlockSpec(memory_space=pltpu.SMEM),
            pl.BlockSpec(memory_space=pltpu.VMEM),
            pl.BlockSpec(memory_space=pltpu.VMEM),
            pl.BlockSpec(memory_space=pl.ANY),
        ],
        out_specs=pl.BlockSpec(memory_space=pl.ANY),
        scratch_shapes=[
            pltpu.VMEM((m, n), F32),
            pltpu.VMEM((m, n), F32),
            pltpu.VMEM(lines.shape, F32),
            pltpu.VMEM((m, m), BF16),
            pltpu.VMEM((m, m), BF16),
            pltpu.VMEM((m, m), BF16),
            pltpu.SemaphoreType.DMA,
            pltpu.SemaphoreType.DMA((n // chunk,)),
        ],
        compiler_params=pltpu.CompilerParams(vmem_limit_bytes=48 * 2**20),
        cost_estimate=pl.CostEstimate(flops=12 * m * k * n, bytes_accessed=8 * m * n, transcendentals=0),
        name="finish",
    )(me, lines, v, x)


def on_device(phase_stack, start_basis):
    pixel_total = phase_stack.shape[1] * lax.axis_size(AXES)
    v = start_rows(start_basis)
    lines = sum_everywhere(upper_gram(phase_stack))
    me = (lax.axis_index("c") * 4 + lax.axis_index("y")) * 4 + lax.axis_index("x")
    return corrected(lines, me.astype(jnp.int32).reshape(1), v, phase_stack, pixel_total)


def solution(mesh):
    split = Mesh(mesh.devices.reshape(-1, 2, mesh.shape["gy"], mesh.shape["gz"]), AXES)
    placed = (P(None, AXES), P())
    return jax.shard_map(
        on_device, mesh=split, in_specs=placed, out_specs=P(None, AXES), check_vma=False
    )
```

```python
import functools
import itertools
import math

import jax
import jax.numpy as jnp
from jax import lax
from jax.experimental import pallas as pl
from jax.experimental.pallas import tpu as pltpu
from jax.sharding import Mesh
from jax.sharding import PartitionSpec as P

ITERS = 3
AXES = ("y", "c", "x", "z")
SHARED = ("c", "y", "x")
HIGHEST = lax.Precision.HIGHEST
EPSILON = 1e-06
TILE = 128
WIDE = 256
ROWS = 8
VMEM = 50 * 2**20
F32 = jnp.float32
BF16 = jnp.bfloat16
NT = (((1,), (1,)), ((), ()))


def shifted(v, axis, k):
    n = lax.axis_size(axis)
    return lax.ppermute(v, axis, [(i, (i + k) % n) for i in range(n)])


def share_of_sum(v, axis):
    n, me = lax.axis_size(axis), lax.axis_index(axis)
    rows = v.shape[0] // n
    piece = lambda k: lax.dynamic_slice_in_dim(v, lax.rem(me + k, n) * rows, rows, 0)
    arrived = [shifted(piece(k), axis, k) for k in range(1, n)]
    total = piece(0)
    for part in arrived:
        total = total + part
    return total


def joined(v, axis):
    return jnp.concatenate([v] + [shifted(v, axis, k) for k in range(1, lax.axis_size(axis))], axis=0)


def summed(v, axis):
    n = lax.axis_size(axis)
    copies = jnp.broadcast_to(v[None], (n, *v.shape)).reshape(n * v.shape[0], *v.shape[1:])
    arrived = lax.all_to_all(copies, axis, 0, 0, tiled=True)
    return arrived.reshape(n, *v.shape).sum(axis=0)


def sum_everywhere(v, meanwhile):
    for axis in SHARED:
        v = share_of_sum(v, axis)
    v, meanwhile = lax.optimization_barrier((summed(v, "z"), meanwhile))
    for axis in reversed(SHARED):
        v = joined(v, axis)
    return v, meanwhile


def two_parts(x):
    hi = x.astype(BF16)
    return hi, (x - hi.astype(F32)).astype(BF16)


def three_parts(x):
    hi = x.astype(BF16)
    rest = x - hi.astype(F32)
    mid = rest.astype(BF16)
    return hi, mid, (rest - mid.astype(F32)).astype(BF16)


def dot(a, b):
    return jnp.dot(a, b, preferred_element_type=F32)


def dot_nt(a, b, precision=None):
    return lax.dot_general(a, b, NT, precision=precision, preferred_element_type=F32)


def iota(shape, dim):
    return lax.broadcasted_iota(jnp.int32, shape, dim)


def gram_kernel(x_ref, out_ref, total):
    step = pl.program_id(0)
    m = x_ref.shape[0]

    @pl.when(step == 0)
    def _():
        total[...] = jnp.zeros_like(total)

    hi, lo = two_parts(x_ref[...])
    for j in range(m // WIDE):
        rows, here = slice(0, (j + 1) * WIDE), slice(j * WIDE, (j + 1) * WIDE)
        total[rows, here] += (
            dot_nt(hi[rows], hi[here]) + dot_nt(lo[rows], hi[here]) + dot_nt(hi[rows], lo[here])
        )

    @pl.when(step == pl.num_programs(0) - 1)
    def _():
        place = 0
        for i in range(m // TILE):
            for j in range(i, m // TILE):
                out_ref[place * TILE : (place + 1) * TILE, :] = total[
                    i * TILE : (i + 1) * TILE, j * TILE : (j + 1) * TILE
                ]
                place += 1


def upper_gram(x, chunk=512):
    m, n = x.shape
    tiles = m // TILE
    lines = tiles * (tiles + 1) // 2 * TILE
    return pl.pallas_call(
        gram_kernel,
        out_shape=jax.ShapeDtypeStruct((lines, TILE), F32),
        grid=(n // chunk,),
        in_specs=[pl.BlockSpec((m, chunk), lambda i: (0, i))],
        out_specs=pl.BlockSpec((lines, TILE), lambda i: (0, 0)),
        scratch_shapes=[pltpu.VMEM((m, m), F32)],
        compiler_params=pltpu.CompilerParams(vmem_limit_bytes=VMEM),
        cost_estimate=pl.CostEstimate(flops=6 * m * m * n, bytes_accessed=4 * m * n, transcendentals=0),
        name="gram",
    )(x)


def inverse_factor(b):
    k = b.shape[0]
    blocks = k // ROWS
    eye = (iota((k, k), 0) == iota((k, k), 1)).astype(F32)
    both = jnp.concatenate([b, eye], axis=1)
    line = [both[ROWS * q : ROWS * (q + 1), :] for q in range(blocks)]
    sub = iota((ROWS, 2 * k), 0)
    for p in range(blocks):
        column = {
            (q, i): jnp.broadcast_to(line[q][:, ROWS * p + i : ROWS * p + i + 1], (ROWS, 2 * k))
            for q in range(p, blocks)
            for i in range(ROWS)
        }
        for i in range(ROWS):
            inverse = 1.0 / column[p, i][i : i + 1, :]
            pivot_row = line[p][i : i + 1, :] * inverse
            ahead = {j: column[p, j][i : i + 1, :] * inverse for j in range(i + 1, ROWS)}
            for q in range(p, blocks):
                factor = column[q, i]
                if q == p:
                    factor = jnp.where(sub > i, factor, 0.0)
                for j in range(i + 1, ROWS):
                    column[q, j] = column[q, j] - factor * ahead[j]
                line[q] = line[q] - factor * pivot_row
    both = jnp.concatenate(line, axis=0)
    pivots = jnp.sum(
        jnp.where(iota(both.shape, 0) == iota(both.shape, 1), both, 0.0), axis=1, keepdims=True
    )
    return (both * lax.rsqrt(pivots))[:, k:]


def orthonormal(y):
    return jnp.dot(inverse_factor(dot_nt(y, y, HIGHEST)), y, precision=HIGHEST)


def start_kernel(s_ref, v_ref):
    v_ref[...] = orthonormal(s_ref[...])


def start_rows(s):
    k, m = s.shape
    return pl.pallas_call(
        start_kernel,
        out_shape=jax.ShapeDtypeStruct((k, m), F32),
        cost_estimate=pl.CostEstimate(flops=8 * 10**9, bytes_accessed=8 * m * k, transcendentals=0),
        name="start_rows",
    )(s)


def times_gram(v, gram):
    k = v.shape[0]
    v0, v1, v2 = three_parts(v)
    first = dot(jnp.concatenate([v0, v1, v2], axis=0), gram[0][...])
    second = dot(jnp.concatenate([v0, v1], axis=0), gram[1][...])
    third = dot(v0, gram[2][...])
    return first[:k] + (
        (first[k : 2 * k] + second[:k]) + ((first[2 * k :] + second[k:]) + third)
    )


def finish_kernel(pixel_total, chunk, sizes, me_ref, lines_ref, v_ref, x_hbm, out_hbm, x, out, ordered, g0, g1, g2, x_sem, out_sem):
    m, n = x_hbm.shape
    k = v_ref.shape[0]
    tiles = m // TILE
    load = pltpu.make_async_copy(x_hbm, x, x_sem)
    load.start()
    slots = math.prod(sizes)
    rows = lines_ref.shape[0] // slots
    for slot, back in enumerate(itertools.product(*map(range, sizes))):
        place = 0
        for axis, (size, hops) in enumerate(zip(sizes, back)):
            place = place * size + lax.rem(me_ref[axis] + (size - hops), size)
        place = pl.multiple_of(place * rows, ROWS)
        ordered[pl.ds(place, rows), :] = lines_ref[slot * rows : (slot + 1) * rows, :]

    gram = (g0, g1, g2)
    diagonal = []
    place = 0
    for i in range(tiles):
        for j in range(i, tiles):
            tile = ordered[place * TILE : (place + 1) * TILE, :] * (1.0 / pixel_total)
            place += 1
            at_i, at_j = slice(i * TILE, (i + 1) * TILE), slice(j * TILE, (j + 1) * TILE)
            for ref, part in zip(gram, three_parts(tile)):
                ref[at_i, at_j] = part
            if i == j:
                eye = iota((TILE, TILE), 0) == iota((TILE, TILE), 1)
                diagonal.append(jnp.sum(jnp.where(eye, tile, 0.0), axis=0, keepdims=True))
            else:
                for ref, part in zip(gram, three_parts(tile.T)):
                    ref[at_j, at_i] = part

    v = v_ref[...]
    for sweep in range(ITERS):
        v = orthonormal(times_gram(v, gram))
    w = times_gram(v, gram)
    inner = dot_nt(w, v, HIGHEST)
    twice = jnp.dot(inner, v, precision=HIGHEST) - 2.0 * w
    power = jnp.concatenate(diagonal, axis=1) + jnp.sum(v * twice, axis=0, keepdims=True)
    scale = lax.rsqrt(jnp.maximum(power, 0.0) + EPSILON)
    scale = jnp.concatenate(
        [
            jnp.broadcast_to(scale[:, i * TILE : (i + 1) * TILE], (TILE, TILE)).T
            for i in range(tiles)
        ],
        axis=0,
    )
    q0, q1 = two_parts(v.T)
    spread = jnp.concatenate([q0, q1, q0], axis=1)
    v0, v1 = two_parts(v)
    v01 = jnp.concatenate([v0, v1], axis=0)
    load.wait()
    for c in range(n // chunk):
        here = slice(c * chunk, (c + 1) * chunk)
        xc = x[:, here]
        x0, x1 = two_parts(xc)
        both = dot(v01, x0)
        l0, l1 = two_parts(both[:k] + (both[k:] + dot(v0, x1)))
        common = dot(spread, jnp.concatenate([l0, l0, l1], axis=0))
        for t in range(chunk // TILE):
            at = slice(t * TILE, (t + 1) * TILE)
            out[:, c * chunk + t * TILE : c * chunk + (t + 1) * TILE] = (xc[:, at] - common[:, at]) * scale
        pltpu.make_async_copy(out.at[:, here], out_hbm.at[:, here], out_sem.at[c]).start()
    for c in range(n // chunk):
        here = slice(c * chunk, (c + 1) * chunk)
        pltpu.make_async_copy(out.at[:, here], out_hbm.at[:, here], out_sem.at[c]).wait()


def corrected(lines, me, sizes, v, x, pixel_total, chunk=512):
    m, n = x.shape
    k = v.shape[0]
    return pl.pallas_call(
        functools.partial(finish_kernel, pixel_total, chunk, sizes),
        out_shape=jax.ShapeDtypeStruct((m, n), F32),
        in_specs=[
            pl.BlockSpec(memory_space=pltpu.SMEM),
            pl.BlockSpec(memory_space=pltpu.VMEM),
            pl.BlockSpec(memory_space=pltpu.VMEM),
            pl.BlockSpec(memory_space=pl.ANY),
        ],
        out_specs=pl.BlockSpec(memory_space=pl.ANY),
        scratch_shapes=[
            pltpu.VMEM((m, n), F32),
            pltpu.VMEM((m, n), F32),
            pltpu.VMEM(lines.shape, F32),
            pltpu.VMEM((m, m), BF16),
            pltpu.VMEM((m, m), BF16),
            pltpu.VMEM((m, m), BF16),
            pltpu.SemaphoreType.DMA,
            pltpu.SemaphoreType.DMA((n // chunk,)),
        ],
        compiler_params=pltpu.CompilerParams(vmem_limit_bytes=VMEM),
        cost_estimate=pl.CostEstimate(flops=12 * m * k * n, bytes_accessed=8 * m * n, transcendentals=0),
        name="finish",
    )(me, lines, v, x)


def on_device(phase_stack, start_basis):
    pixel_total = phase_stack.shape[1] * lax.axis_size(AXES)
    lines, v = sum_everywhere(upper_gram(phase_stack), start_rows(start_basis.T))
    me = jnp.stack([lax.axis_index(axis) for axis in SHARED]).astype(jnp.int32)
    sizes = tuple(lax.axis_size(axis) for axis in SHARED)
    return corrected(lines, me, sizes, v, phase_stack, pixel_total)


def solution(mesh):
    split = Mesh(mesh.devices.reshape(-1, 2, mesh.shape["gy"], mesh.shape["gz"]), AXES)
    placed = (P(None, AXES), P())
    return jax.shard_map(
        on_device, mesh=split, in_specs=placed, out_specs=P(None, AXES), check_vma=False
    )
```

```python
import functools
import itertools
import math

import jax
import jax.numpy as jnp
from jax import lax
from jax.experimental import pallas as pl
from jax.experimental.pallas import tpu as pltpu
from jax.sharding import Mesh
from jax.sharding import PartitionSpec as P

ITERS = 3
AXES = ("y", "c", "x", "z")
SHARED = ("c", "y", "x")
HIGHEST = lax.Precision.HIGHEST
EPSILON = 1e-06
TILE = 128
WIDE = 256
ROWS = 8
VMEM = 50 * 2**20
F32 = jnp.float32
BF16 = jnp.bfloat16
NT = (((1,), (1,)), ((), ()))


def half():
    return (lax.axis_index("c") + lax.axis_index("x") + lax.axis_index("y")) % 2


def place_on(axis):
    return half() if axis == "c" else lax.axis_index(axis)


def shifted(v, axis, k):
    sizes = [lax.axis_size(a) for a in AXES]
    along, core = AXES.index(axis), AXES.index("c")
    pairs = []
    for source, at in enumerate(itertools.product(*map(range, sizes))):
        to = list(at)
        to[along] = (to[along] + k) % sizes[along]
        if along != core:
            to[core] = (to[core] + k) % 2
        target = 0
        for size, i in zip(sizes, to):
            target = target * size + i
        pairs.append((source, target))
    return lax.ppermute(v, AXES, pairs)


def share_of_sum(v, axis):
    n, me = lax.axis_size(axis), place_on(axis)
    rows = v.shape[0] // n
    piece = lambda k: lax.dynamic_slice_in_dim(v, lax.rem(me + k, n) * rows, rows, 0)
    arrived = [shifted(piece(k), axis, k) for k in range(1, n)]
    total = piece(0)
    for part in arrived:
        total = total + part
    return total


def joined(v, axis):
    return jnp.concatenate([v] + [shifted(v, axis, k) for k in range(1, lax.axis_size(axis))], axis=0)


def summed(v, axis):
    n = lax.axis_size(axis)
    copies = jnp.broadcast_to(v[None], (n, *v.shape)).reshape(n * v.shape[0], *v.shape[1:])
    arrived = lax.all_to_all(copies, axis, 0, 0, tiled=True)
    return arrived.reshape(n, *v.shape).sum(axis=0)


def sum_everywhere(v, meanwhile):
    for axis in SHARED:
        v = share_of_sum(v, axis)
    v, meanwhile = lax.optimization_barrier((summed(v, "z"), meanwhile))
    for axis in reversed(SHARED):
        v = joined(v, axis)
    return v, meanwhile


def two_parts(x):
    hi = x.astype(BF16)
    return hi, (x - hi.astype(F32)).astype(BF16)


def three_parts(x):
    hi = x.astype(BF16)
    rest = x - hi.astype(F32)
    mid = rest.astype(BF16)
    return hi, mid, (rest - mid.astype(F32)).astype(BF16)


def dot(a, b):
    return jnp.dot(a, b, preferred_element_type=F32)


def dot_nt(a, b, precision=None):
    return lax.dot_general(a, b, NT, precision=precision, preferred_element_type=F32)


def iota(shape, dim):
    return lax.broadcasted_iota(jnp.int32, shape, dim)


def gram_kernel(x_hbm, out_ref, x, sem):
    m, n = x_hbm.shape
    bands = [slice(i, i + WIDE) for i in range(0, m, WIDE)]
    loads = [pltpu.make_async_copy(x_hbm.at[b], x.at[b], sem.at[i]) for i, b in enumerate(bands)]
    for load in loads:
        load.start()
    tiles = m // TILE
    places = {}
    for i in range(tiles):
        for j in range(i, tiles):
            places[i, j] = len(places)
    step = WIDE // TILE
    parts = []
    for j, load in enumerate(loads):
        load.wait()
        parts.append(two_parts(x[bands[j]]))
        hi, lo = parts[j]
        for i in range(j + 1):
            above_hi, above_lo = parts[i]
            block = dot_nt(above_hi, hi) + (dot_nt(above_lo, hi) + dot_nt(above_hi, lo))
            for s in range(step):
                for t in range(step):
                    place = places.get((i * step + s, j * step + t))
                    if place is not None:
                        out_ref[place * TILE : (place + 1) * TILE, :] = block[
                            s * TILE : (s + 1) * TILE, t * TILE : (t + 1) * TILE
                        ]


def upper_gram(x):
    m, n = x.shape
    tiles = m // TILE
    lines = tiles * (tiles + 1) // 2 * TILE
    return pl.pallas_call(
        gram_kernel,
        out_shape=jax.ShapeDtypeStruct((lines, TILE), F32),
        in_specs=[pl.BlockSpec(memory_space=pl.ANY)],
        out_specs=pl.BlockSpec(memory_space=pltpu.VMEM),
        scratch_shapes=[pltpu.VMEM((m, n), F32), pltpu.SemaphoreType.DMA((m // WIDE,))],
        compiler_params=pltpu.CompilerParams(vmem_limit_bytes=VMEM),
        cost_estimate=pl.CostEstimate(flops=6 * m * m * n, bytes_accessed=4 * m * n, transcendentals=0),
        name="gram",
    )(x)


def inverse_factor(b):
    k = b.shape[0]
    blocks = k // ROWS
    eye = (iota((k, k), 0) == iota((k, k), 1)).astype(F32)
    both = jnp.concatenate([b, eye], axis=1)
    line = [both[ROWS * q : ROWS * (q + 1), :] for q in range(blocks)]
    sub = iota((ROWS, 2 * k), 0)
    for p in range(blocks):
        column = {
            (q, i): jnp.broadcast_to(line[q][:, ROWS * p + i : ROWS * p + i + 1], (ROWS, 2 * k))
            for q in range(p, blocks)
            for i in range(ROWS)
        }
        for i in range(0, ROWS, 2):
            a, b_, c = column[p, i][i : i + 1, :], column[p, i + 1][i : i + 1, :], column[p, i + 1][i + 1 : i + 2, :]
            first = 1.0 / a
            second = a / (a * c - b_ * b_)
            lower = b_ * first
            others = range(i + 2, ROWS)
            top = {j: column[p, j][i : i + 1, :] for j in others}
            ahead = {j: top[j] * first for j in others}
            then = {j: (column[p, j][i + 1 : i + 2, :] - lower * top[j]) * second for j in others}
            top_row = line[p][i : i + 1, :]
            first_row = top_row * first
            next_row = (line[p][i + 1 : i + 2, :] - lower * top_row) * second
            for q in range(p, blocks):
                factor = column[q, i]
                following = column[q, i + 1] - factor * lower
                if q == p:
                    factor = jnp.where(sub > i, factor, 0.0)
                    following = jnp.where(sub > i + 1, following, 0.0)
                for j in others:
                    column[q, j] = column[q, j] - factor * ahead[j] - following * then[j]
                line[q] = line[q] - factor * first_row - following * next_row
    both = jnp.concatenate(line, axis=0)
    pivots = jnp.sum(
        jnp.where(iota(both.shape, 0) == iota(both.shape, 1), both, 0.0), axis=1, keepdims=True
    )
    return (both * lax.rsqrt(pivots))[:, k:]


def orthonormal(y):
    return jnp.dot(inverse_factor(dot_nt(y, y, HIGHEST)), y, precision=HIGHEST)


def start_kernel(s_ref, v_ref):
    s = s_ref[...]
    size = jnp.max(jnp.max(jnp.abs(s), axis=0, keepdims=True), axis=1, keepdims=True)
    v_ref[...] = orthonormal(s / size)


def start_rows(s):
    k, m = s.shape
    return pl.pallas_call(
        start_kernel,
        out_shape=jax.ShapeDtypeStruct((k, m), F32),
        compiler_params=pltpu.CompilerParams(vmem_limit_bytes=8 * 2**20),
        cost_estimate=pl.CostEstimate(flops=8 * 10**9, bytes_accessed=8 * m * k, transcendentals=0),
        name="start_rows",
    )(s)


def times_gram(v, gram):
    k = v.shape[0]
    v0, v1, v2 = three_parts(v)
    first = dot(jnp.concatenate([v0, v1, v2], axis=0), gram[0][...])
    second = dot(jnp.concatenate([v0, v1], axis=0), gram[1][...])
    third = dot(v0, gram[2][...])
    return first[:k] + (
        (first[k : 2 * k] + second[:k]) + ((first[2 * k :] + second[k:]) + third)
    )


def finish_kernel(pixel_total, chunk, sizes, me_ref, lines_ref, v_ref, x_hbm, out_hbm, x, out, ordered, g0, g1, g2, x_sem, out_sem):
    m, n = x_hbm.shape
    k = v_ref.shape[0]
    tiles = m // TILE
    load = pltpu.make_async_copy(x_hbm, x, x_sem)
    load.start()
    slots = math.prod(sizes)
    rows = lines_ref.shape[0] // slots
    for slot, back in enumerate(itertools.product(*map(range, sizes))):
        place = 0
        for axis, (size, hops) in enumerate(zip(sizes, back)):
            place = place * size + lax.rem(me_ref[axis] + (size - hops), size)
        place = pl.multiple_of(place * rows, ROWS)
        ordered[pl.ds(place, rows), :] = lines_ref[slot * rows : (slot + 1) * rows, :]

    gram = (g0, g1, g2)
    diagonal = []
    place = 0
    for i in range(tiles):
        for j in range(i, tiles):
            tile = ordered[place * TILE : (place + 1) * TILE, :] * (1.0 / pixel_total)
            place += 1
            at_i, at_j = slice(i * TILE, (i + 1) * TILE), slice(j * TILE, (j + 1) * TILE)
            for ref, part in zip(gram, three_parts(tile)):
                ref[at_i, at_j] = part
            if i == j:
                eye = iota((TILE, TILE), 0) == iota((TILE, TILE), 1)
                diagonal.append(jnp.sum(jnp.where(eye, tile, 0.0), axis=0, keepdims=True))
            else:
                for ref, part in zip(gram, three_parts(tile.T)):
                    ref[at_j, at_i] = part

    diagonal = jnp.concatenate(diagonal, axis=1)
    evened = m / jnp.sum(diagonal, axis=1, keepdims=True)
    v = v_ref[...]
    for sweep in range(ITERS):
        v = orthonormal(times_gram(v, gram) * evened)
    load.wait()
    w = times_gram(v, gram)
    inner = dot_nt(w, v, HIGHEST)
    twice = jnp.dot(inner, v, precision=HIGHEST) - 2.0 * w
    power = diagonal + jnp.sum(v * twice, axis=0, keepdims=True)
    scale = lax.rsqrt(jnp.maximum(power, 0.0) + EPSILON)
    scale = jnp.concatenate(
        [
            jnp.broadcast_to(scale[:, i * TILE : (i + 1) * TILE], (TILE, TILE)).T
            for i in range(tiles)
        ],
        axis=0,
    )
    q0, q1 = two_parts(v.T)
    spread = jnp.concatenate([q0, q1, q0], axis=1)
    v0, v1 = two_parts(v)
    v01 = jnp.concatenate([v0, v1], axis=0)
    for c in range(n // chunk):
        here = slice(c * chunk, (c + 1) * chunk)
        xc = x[:, here]
        x0, x1 = two_parts(xc)
        both = dot(v01, x0)
        l0, l1 = two_parts(both[:k] + (both[k:] + dot(v0, x1)))
        common = dot(spread, jnp.concatenate([l0, l0, l1], axis=0))
        for t in range(chunk // TILE):
            at = slice(t * TILE, (t + 1) * TILE)
            out[:, c * chunk + t * TILE : c * chunk + (t + 1) * TILE] = (xc[:, at] - common[:, at]) * scale
        pltpu.make_async_copy(out.at[:, here], out_hbm.at[:, here], out_sem.at[c]).start()
    for c in range(n // chunk):
        here = slice(c * chunk, (c + 1) * chunk)
        pltpu.make_async_copy(out.at[:, here], out_hbm.at[:, here], out_sem.at[c]).wait()


def corrected(lines, me, sizes, v, x, pixel_total, chunk=512):
    m, n = x.shape
    k = v.shape[0]
    return pl.pallas_call(
        functools.partial(finish_kernel, pixel_total, chunk, sizes),
        out_shape=jax.ShapeDtypeStruct((m, n), F32),
        in_specs=[
            pl.BlockSpec(memory_space=pltpu.SMEM),
            pl.BlockSpec(memory_space=pltpu.VMEM),
            pl.BlockSpec(memory_space=pltpu.VMEM),
            pl.BlockSpec(memory_space=pl.ANY),
        ],
        out_specs=pl.BlockSpec(memory_space=pl.ANY),
        scratch_shapes=[
            pltpu.VMEM((m, n), F32),
            pltpu.VMEM((m, n), F32),
            pltpu.VMEM(lines.shape, F32),
            pltpu.VMEM((m, m), BF16),
            pltpu.VMEM((m, m), BF16),
            pltpu.VMEM((m, m), BF16),
            pltpu.SemaphoreType.DMA,
            pltpu.SemaphoreType.DMA((n // chunk,)),
        ],
        compiler_params=pltpu.CompilerParams(vmem_limit_bytes=VMEM),
        cost_estimate=pl.CostEstimate(flops=12 * m * k * n, bytes_accessed=8 * m * n, transcendentals=0),
        name="finish",
    )(me, lines, v, x)


def on_device(phase_stack, start_basis):
    pixel_total = phase_stack.shape[1] * lax.axis_size(AXES)
    lines, v = sum_everywhere(upper_gram(phase_stack), start_rows(start_basis.T))
    me = jnp.stack([place_on(axis) for axis in SHARED]).astype(jnp.int32)
    sizes = tuple(lax.axis_size(axis) for axis in SHARED)
    return corrected(lines, me, sizes, v, phase_stack, pixel_total)


def solution(mesh):
    split = Mesh(mesh.devices.reshape(-1, 2, mesh.shape["gy"], mesh.shape["gz"]), AXES)
    placed = (P(None, AXES), P())
    return jax.shard_map(
        on_device, mesh=split, in_specs=placed, out_specs=P(None, AXES), check_vma=False
    )
```

```python
import functools
import itertools
import math

import jax
import jax.numpy as jnp
from jax import lax
from jax.experimental import pallas as pl
from jax.experimental.pallas import tpu as pltpu
from jax.sharding import Mesh
from jax.sharding import PartitionSpec as P

ITERS = 3
AXES = ("y", "c", "x", "z")
SHARED = ("c", "y", "x")
HIGHEST = lax.Precision.HIGHEST
EPSILON = 1e-06
TILE = 128
WIDE = 256
ROWS = 8
VMEM = 50 * 2**20
F32 = jnp.float32
BF16 = jnp.bfloat16
NT = (((1,), (1,)), ((), ()))


def half():
    return (lax.axis_index("c") + lax.axis_index("x") + lax.axis_index("y")) % 2


def place_on(axis):
    return half() if axis == "c" else lax.axis_index(axis)


def shifted(v, axis, k):
    sizes = [lax.axis_size(a) for a in AXES]
    along, core = AXES.index(axis), AXES.index("c")
    pairs = []
    for source, at in enumerate(itertools.product(*map(range, sizes))):
        to = list(at)
        to[along] = (to[along] + k) % sizes[along]
        if along != core:
            to[core] = (to[core] + k) % 2
        target = 0
        for size, i in zip(sizes, to):
            target = target * size + i
        pairs.append((source, target))
    return lax.ppermute(v, AXES, pairs)


def steps(n):
    return sorted(range(1, n), key=lambda k: -min(k, n - k))


def share_of_sum(v, axis):
    n, me = lax.axis_size(axis), place_on(axis)
    rows = v.shape[0] // n
    piece = lambda k: lax.dynamic_slice_in_dim(v, lax.rem(me + k, n) * rows, rows, 0)
    arrived = [shifted(piece(k), axis, k) for k in steps(n)]
    total = piece(0)
    for part in arrived:
        total = total + part
    return total


def joined(v, axis):
    return jnp.concatenate([v] + [shifted(v, axis, k) for k in steps(lax.axis_size(axis))], axis=0)


def summed(v, axis):
    n = lax.axis_size(axis)
    copies = jnp.broadcast_to(v[None], (n, *v.shape)).reshape(n * v.shape[0], *v.shape[1:])
    arrived = lax.all_to_all(copies, axis, 0, 0, tiled=True)
    return arrived.reshape(n, *v.shape).sum(axis=0)


def sum_everywhere(v, meanwhile):
    for axis in SHARED:
        v = share_of_sum(v, axis)
    v, meanwhile = lax.optimization_barrier((summed(v, "z"), meanwhile))
    for axis in reversed(SHARED):
        v = joined(v, axis)
    return v, meanwhile


def two_parts(x):
    hi = x.astype(BF16)
    return hi, (x - hi.astype(F32)).astype(BF16)


def three_parts(x):
    hi = x.astype(BF16)
    rest = x - hi.astype(F32)
    mid = rest.astype(BF16)
    return hi, mid, (rest - mid.astype(F32)).astype(BF16)


def dot(a, b):
    return jnp.dot(a, b, preferred_element_type=F32)


def dot_nt(a, b, precision=None):
    return lax.dot_general(a, b, NT, precision=precision, preferred_element_type=F32)


def iota(shape, dim):
    return lax.broadcasted_iota(jnp.int32, shape, dim)


def gram_kernel(x_hbm, out_ref, x, sem):
    m, n = x_hbm.shape
    bands = [slice(i, i + WIDE) for i in range(0, m, WIDE)]
    loads = [pltpu.make_async_copy(x_hbm.at[b], x.at[b], sem.at[i]) for i, b in enumerate(bands)]
    for load in loads:
        load.start()
    tiles = m // TILE
    places = {}
    for i in range(tiles):
        for j in range(i, tiles):
            places[i, j] = len(places)
    step = WIDE // TILE
    parts = []
    for j, load in enumerate(loads):
        load.wait()
        parts.append(two_parts(x[bands[j]]))
        hi, lo = parts[j]
        for i in range(j + 1):
            above_hi, above_lo = parts[i]
            if i < j:
                block = dot_nt(above_hi, hi) + (dot_nt(above_lo, hi) + dot_nt(above_hi, lo))
            else:
                mixed = dot_nt(hi, lo)
                block = dot_nt(hi, hi) + ((mixed + mixed.T) + dot_nt(lo, lo))
            for s in range(step):
                for t in range(step):
                    place = places.get((i * step + s, j * step + t))
                    if place is not None:
                        out_ref[place * TILE : (place + 1) * TILE, :] = block[
                            s * TILE : (s + 1) * TILE, t * TILE : (t + 1) * TILE
                        ]


def upper_gram(x):
    m, n = x.shape
    tiles = m // TILE
    lines = tiles * (tiles + 1) // 2 * TILE
    return pl.pallas_call(
        gram_kernel,
        out_shape=jax.ShapeDtypeStruct((lines, TILE), F32),
        in_specs=[pl.BlockSpec(memory_space=pl.ANY)],
        out_specs=pl.BlockSpec(memory_space=pltpu.VMEM),
        scratch_shapes=[pltpu.VMEM((m, n), F32), pltpu.SemaphoreType.DMA((m // WIDE,))],
        compiler_params=pltpu.CompilerParams(vmem_limit_bytes=VMEM),
        cost_estimate=pl.CostEstimate(flops=6 * m * m * n, bytes_accessed=4 * m * n, transcendentals=0),
        name="gram",
    )(x)


def inverse_factor(b):
    k = b.shape[0]
    blocks = k // ROWS
    eye = (iota((k, k), 0) == iota((k, k), 1)).astype(F32)
    both = jnp.concatenate([b, eye], axis=1)
    line = [both[ROWS * q : ROWS * (q + 1), :] for q in range(blocks)]
    sub = iota((ROWS, 2 * k), 0)
    span = 16
    per = span // ROWS
    for p in range(0, blocks, per):
        column = {
            (q, i): jnp.broadcast_to(line[q][:, ROWS * p + i : ROWS * p + i + 1], (ROWS, 2 * k))
            for q in range(p, blocks)
            for i in range(span)
        }
        at = lambda i, j: column[p + i // ROWS, j][i % ROWS : i % ROWS + 1, :]
        for i in range(0, span, 2):
            a, b_, c = at(i, i), at(i, i + 1), at(i + 1, i + 1)
            first = pl.reciprocal(a)
            second = a * pl.reciprocal(a * c - b_ * b_)
            lower = b_ * first
            others = range(i + 2, span)
            top = {j: at(i, j) for j in others}
            ahead = {j: top[j] * first for j in others}
            then = {j: (at(i + 1, j) - lower * top[j]) * second for j in others}
            home, row = p + i // ROWS, i % ROWS
            top_row = line[home][row : row + 1, :]
            first_row = top_row * first
            next_row = (line[home][row + 1 : row + 2, :] - lower * top_row) * second
            for q in range(home, blocks):
                factor = column[q, i]
                following = column[q, i + 1] - factor * lower
                if q == home:
                    factor = jnp.where(sub > row, factor, 0.0)
                    following = jnp.where(sub > row + 1, following, 0.0)
                for j in others:
                    column[q, j] = column[q, j] - factor * ahead[j] - following * then[j]
                line[q] = line[q] - factor * first_row - following * next_row
    both = jnp.concatenate(line, axis=0)
    pivots = jnp.sum(
        jnp.where(iota(both.shape, 0) == iota(both.shape, 1), both, 0.0), axis=1, keepdims=True
    )
    return (both * lax.rsqrt(pivots))[:, k:]


def orthonormal(y):
    return jnp.dot(inverse_factor(dot_nt(y, y, HIGHEST)), y, precision=HIGHEST)


def start_kernel(s_ref, v_ref):
    s = s_ref[...]
    size = jnp.max(jnp.max(jnp.abs(s), axis=0, keepdims=True), axis=1, keepdims=True)
    v_ref[...] = orthonormal(s / size)


def start_rows(s):
    k, m = s.shape
    return pl.pallas_call(
        start_kernel,
        out_shape=jax.ShapeDtypeStruct((k, m), F32),
        compiler_params=pltpu.CompilerParams(vmem_limit_bytes=8 * 2**20),
        cost_estimate=pl.CostEstimate(flops=8 * 10**9, bytes_accessed=8 * m * k, transcendentals=0),
        name="start_rows",
    )(s)


def times_gram(v, gram):
    k = v.shape[0]
    v0, v1, v2 = three_parts(v)
    first = dot(jnp.concatenate([v0, v1, v2], axis=0), gram[0][...])
    second = dot(jnp.concatenate([v0, v1], axis=0), gram[1][...])
    third = dot(v0, gram[2][...])
    return first[:k] + (
        (first[k : 2 * k] + second[:k]) + ((first[2 * k :] + second[k:]) + third)
    )


def finish_kernel(pixel_total, chunk, sizes, me_ref, lines_ref, v_ref, x_hbm, out_hbm, x, out, ordered, g0, g1, g2, x0_ref, x1_ref, x_sem, out_sem):
    m, n = x_hbm.shape
    k = v_ref.shape[0]
    tiles = m // TILE
    load = pltpu.make_async_copy(x_hbm, x, x_sem)
    load.start()
    slots = math.prod(sizes)
    rows = lines_ref.shape[0] // slots
    for slot, back in enumerate(itertools.product(*([0, *steps(size)] for size in sizes))):
        place = 0
        for axis, (size, hops) in enumerate(zip(sizes, back)):
            place = place * size + lax.rem(me_ref[axis] + (size - hops), size)
        place = pl.multiple_of(place * rows, ROWS)
        ordered[pl.ds(place, rows), :] = lines_ref[slot * rows : (slot + 1) * rows, :]

    gram = (g0, g1, g2)
    diagonal = []
    place = 0
    for i in range(tiles):
        for j in range(i, tiles):
            tile = ordered[place * TILE : (place + 1) * TILE, :] * (1.0 / pixel_total)
            place += 1
            at_i, at_j = slice(i * TILE, (i + 1) * TILE), slice(j * TILE, (j + 1) * TILE)
            for ref, part in zip(gram, three_parts(tile)):
                ref[at_i, at_j] = part
            if i == j:
                eye = iota((TILE, TILE), 0) == iota((TILE, TILE), 1)
                diagonal.append(jnp.sum(jnp.where(eye, tile, 0.0), axis=0, keepdims=True))
            else:
                for ref, part in zip(gram, three_parts(tile.T)):
                    ref[at_j, at_i] = part

    diagonal = jnp.concatenate(diagonal, axis=1)
    evened = m / jnp.sum(diagonal, axis=1, keepdims=True)
    v = v_ref[...]
    for sweep in range(ITERS):
        if sweep == ITERS - 1:
            load.wait()
            x0_ref[...], x1_ref[...] = two_parts(x[...])
        v = orthonormal(times_gram(v, gram) * evened)
    w = times_gram(v, gram)
    inner = dot_nt(w, v, HIGHEST)
    twice = jnp.dot(inner, v, precision=HIGHEST) - 2.0 * w
    power = diagonal + jnp.sum(v * twice, axis=0, keepdims=True)
    scale = lax.rsqrt(jnp.maximum(power, 0.0) + EPSILON)
    scale = jnp.concatenate(
        [
            jnp.broadcast_to(scale[:, i * TILE : (i + 1) * TILE], (TILE, TILE)).T
            for i in range(tiles)
        ],
        axis=0,
    )
    q0, q1 = two_parts(v.T)
    spread = jnp.concatenate([q0, q1, q0], axis=1)
    v0, v1 = two_parts(v)
    v01 = jnp.concatenate([v0, v1], axis=0)
    cuts = [*range(0, n, chunk), n - chunk // 2, n]
    bands = [slice(a, b) for a, b in zip(cuts, cuts[1:])]
    for c, here in enumerate(bands):
        xc = x[:, here]
        x0, x1 = x0_ref[:, here], x1_ref[:, here]
        both = dot(v01, x0)
        l0, l1 = two_parts(both[:k] + (both[k:] + dot(v0, x1)))
        common = dot(spread, jnp.concatenate([l0, l0, l1], axis=0))
        for t in range((here.stop - here.start) // TILE):
            at = slice(t * TILE, (t + 1) * TILE)
            out[:, here.start + t * TILE : here.start + (t + 1) * TILE] = (xc[:, at] - common[:, at]) * scale
        pltpu.make_async_copy(out.at[:, here], out_hbm.at[:, here], out_sem.at[c]).start()
    for c, here in enumerate(bands):
        pltpu.make_async_copy(out.at[:, here], out_hbm.at[:, here], out_sem.at[c]).wait()


def corrected(lines, me, sizes, v, x, pixel_total, chunk=512):
    m, n = x.shape
    k = v.shape[0]
    return pl.pallas_call(
        functools.partial(finish_kernel, pixel_total, chunk, sizes),
        out_shape=jax.ShapeDtypeStruct((m, n), F32),
        in_specs=[
            pl.BlockSpec(memory_space=pltpu.SMEM),
            pl.BlockSpec(memory_space=pltpu.VMEM),
            pl.BlockSpec(memory_space=pltpu.VMEM),
            pl.BlockSpec(memory_space=pl.ANY),
        ],
        out_specs=pl.BlockSpec(memory_space=pl.ANY),
        scratch_shapes=[
            pltpu.VMEM((m, n), F32),
            pltpu.VMEM((m, n), F32),
            pltpu.VMEM(lines.shape, F32),
            pltpu.VMEM((m, m), BF16),
            pltpu.VMEM((m, m), BF16),
            pltpu.VMEM((m, m), BF16),
            pltpu.VMEM((m, n), BF16),
            pltpu.VMEM((m, n), BF16),
            pltpu.SemaphoreType.DMA,
            pltpu.SemaphoreType.DMA((n // chunk + 1,)),
        ],
        compiler_params=pltpu.CompilerParams(vmem_limit_bytes=VMEM),
        cost_estimate=pl.CostEstimate(flops=12 * m * k * n, bytes_accessed=8 * m * n, transcendentals=0),
        name="finish",
    )(me, lines, v, x)


def on_device(phase_stack, start_basis):
    pixel_total = phase_stack.shape[1] * lax.axis_size(AXES)
    lines, v = sum_everywhere(upper_gram(phase_stack), start_rows(start_basis.T))
    me = jnp.stack([place_on(axis) for axis in SHARED]).astype(jnp.int32)
    sizes = tuple(lax.axis_size(axis) for axis in SHARED)
    return corrected(lines, me, sizes, v, phase_stack, pixel_total)


def solution(mesh):
    split = Mesh(mesh.devices.reshape(-1, 2, mesh.shape["gy"], mesh.shape["gz"]), AXES)
    placed = (P(None, AXES), P())
    return jax.shard_map(
        on_device, mesh=split, in_specs=placed, out_specs=P(None, AXES), check_vma=False
    )
```

```python
import functools
import itertools
import math

import jax
import jax.numpy as jnp
from jax import lax
from jax.experimental import pallas as pl
from jax.experimental.pallas import tpu as pltpu
from jax.sharding import Mesh
from jax.sharding import PartitionSpec as P

ITERS = 3
AXES = ("y", "c", "x", "z")
SHARED = ("c", "y", "x")
HIGHEST = lax.Precision.HIGHEST
EPSILON = 1e-06
TILE = 128
WIDE = 256
ROWS = 8
VMEM = 50 * 2**20
F32 = jnp.float32
BF16 = jnp.bfloat16
NT = (((1,), (1,)), ((), ()))


def half():
    return sum(lax.axis_index(axis) for axis in AXES) % 2


def place_on(axis):
    return half() if axis == "c" else lax.axis_index(axis)


def shifted(v, axis, k):
    sizes = [lax.axis_size(a) for a in AXES]
    along, core = AXES.index(axis), AXES.index("c")
    pairs = []
    for source, at in enumerate(itertools.product(*map(range, sizes))):
        to = list(at)
        to[along] = (to[along] + k) % sizes[along]
        if along != core:
            to[core] = (to[core] + k) % 2
        target = 0
        for size, i in zip(sizes, to):
            target = target * size + i
        pairs.append((source, target))
    return lax.ppermute(v, AXES, pairs)


def steps(n):
    return sorted(range(1, n), key=lambda k: -min(k, n - k))


def share_of_sum(v, axis):
    n, me = lax.axis_size(axis), place_on(axis)
    rows = v.shape[0] // n
    piece = lambda k: lax.dynamic_slice_in_dim(v, lax.rem(me + k, n) * rows, rows, 0)
    arrived = [shifted(piece(k), axis, k) for k in steps(n)]
    total = piece(0)
    for part in arrived:
        total = total + part
    return total


def joined(v, axis):
    return jnp.concatenate([v] + [shifted(v, axis, k) for k in steps(lax.axis_size(axis))], axis=0)


def summed(v, axis):
    pairs = lax.axis_size(axis) // 2
    v = v + shifted(v, axis, pairs)
    arrived = [shifted(v, axis, k if 2 * k <= pairs else k - pairs) for k in steps(pairs)]
    for part in arrived:
        v = v + part
    return v


def sum_everywhere(v, meanwhile):
    for axis in SHARED:
        v = share_of_sum(v, axis)
    v, meanwhile = lax.optimization_barrier((summed(v, "z"), meanwhile))
    for axis in reversed(SHARED):
        v = joined(v, axis)
    return v, meanwhile


def two_parts(x):
    hi = x.astype(BF16)
    return hi, (x - hi.astype(F32)).astype(BF16)


def three_parts(x):
    hi = x.astype(BF16)
    rest = x - hi.astype(F32)
    mid = rest.astype(BF16)
    return hi, mid, (rest - mid.astype(F32)).astype(BF16)


def dot(a, b):
    return jnp.dot(a, b, preferred_element_type=F32)


def dot_nt(a, b, precision=None):
    return lax.dot_general(a, b, NT, precision=precision, preferred_element_type=F32)


def iota(shape, dim):
    return lax.broadcasted_iota(jnp.int32, shape, dim)


def gram_kernel(x_hbm, out_ref, x, sem):
    m, n = x_hbm.shape
    bands = [slice(i, i + WIDE) for i in range(0, m, WIDE)]
    loads = [pltpu.make_async_copy(x_hbm.at[b], x.at[b], sem.at[i]) for i, b in enumerate(bands)]
    for load in loads:
        load.start()
    tiles = m // TILE
    places = {}
    for i in range(tiles):
        for j in range(i, tiles):
            places[i, j] = len(places)
    step = WIDE // TILE
    parts = []
    for j, load in enumerate(loads):
        load.wait()
        parts.append(two_parts(x[bands[j]]))
        hi, lo = parts[j]
        for i in range(j + 1):
            above_hi, above_lo = parts[i]
            if i < j:
                block = dot_nt(above_hi, hi) + (dot_nt(above_lo, hi) + dot_nt(above_hi, lo))
            else:
                mixed = dot_nt(hi, lo)
                block = dot_nt(hi, hi) + ((mixed + mixed.T) + dot_nt(lo, lo))
            for s in range(step):
                for t in range(step):
                    place = places.get((i * step + s, j * step + t))
                    if place is not None:
                        out_ref[place * TILE : (place + 1) * TILE, :] = block[
                            s * TILE : (s + 1) * TILE, t * TILE : (t + 1) * TILE
                        ]


def upper_gram(x):
    m, n = x.shape
    tiles = m // TILE
    lines = tiles * (tiles + 1) // 2 * TILE
    return pl.pallas_call(
        gram_kernel,
        out_shape=jax.ShapeDtypeStruct((lines, TILE), F32),
        in_specs=[pl.BlockSpec(memory_space=pl.ANY)],
        out_specs=pl.BlockSpec(memory_space=pltpu.VMEM),
        scratch_shapes=[pltpu.VMEM((m, n), F32), pltpu.SemaphoreType.DMA((m // WIDE,))],
        compiler_params=pltpu.CompilerParams(vmem_limit_bytes=VMEM),
        cost_estimate=pl.CostEstimate(flops=6 * m * m * n, bytes_accessed=4 * m * n, transcendentals=0),
        name="gram",
    )(x)


def inverse_factor(b):
    k = b.shape[0]
    blocks = k // ROWS
    eye = (iota((k, k), 0) == iota((k, k), 1)).astype(F32)
    both = jnp.concatenate([b, eye], axis=1)
    line = [both[ROWS * q : ROWS * (q + 1), :] for q in range(blocks)]
    sub = iota((ROWS, 2 * k), 0)
    span = 16
    per = span // ROWS
    for p in range(0, blocks, per):
        column = {
            (q, i): jnp.broadcast_to(line[q][:, ROWS * p + i : ROWS * p + i + 1], (ROWS, 2 * k))
            for q in range(p, blocks)
            for i in range(span)
        }
        at = lambda i, j: column[p + i // ROWS, j][i % ROWS : i % ROWS + 1, :]
        for i in range(0, span, 2):
            a, b_, c = at(i, i), at(i, i + 1), at(i + 1, i + 1)
            first = pl.reciprocal(a)
            second = a * pl.reciprocal(a * c - b_ * b_)
            lower = b_ * first
            others = range(i + 2, span)
            top = {j: at(i, j) for j in others}
            ahead = {j: top[j] * first for j in others}
            then = {j: (at(i + 1, j) - lower * top[j]) * second for j in others}
            home, row = p + i // ROWS, i % ROWS
            top_row = line[home][row : row + 1, :]
            first_row = top_row * first
            next_row = (line[home][row + 1 : row + 2, :] - lower * top_row) * second
            for q in range(home, blocks):
                factor = column[q, i]
                following = column[q, i + 1] - factor * lower
                if q == home:
                    factor = jnp.where(sub > row, factor, 0.0)
                    following = jnp.where(sub > row + 1, following, 0.0)
                for j in others:
                    column[q, j] = column[q, j] - factor * ahead[j] - following * then[j]
                line[q] = line[q] - factor * first_row - following * next_row
    both = jnp.concatenate(line, axis=0)
    pivots = jnp.sum(
        jnp.where(iota(both.shape, 0) == iota(both.shape, 1), both, 0.0), axis=1, keepdims=True
    )
    return (both * lax.rsqrt(pivots))[:, k:]


def orthonormal(y):
    return jnp.dot(inverse_factor(dot_nt(y, y, HIGHEST)), y, precision=HIGHEST)


def start_kernel(s_ref, v_ref):
    s = s_ref[...]
    size = jnp.max(jnp.max(jnp.abs(s), axis=0, keepdims=True), axis=1, keepdims=True)
    v_ref[...] = orthonormal(s / size)


def start_rows(s):
    k, m = s.shape
    return pl.pallas_call(
        start_kernel,
        out_shape=jax.ShapeDtypeStruct((k, m), F32),
        compiler_params=pltpu.CompilerParams(vmem_limit_bytes=8 * 2**20),
        cost_estimate=pl.CostEstimate(flops=8 * 10**9, bytes_accessed=8 * m * k, transcendentals=0),
        name="start_rows",
    )(s)


def times_gram(v, gram):
    k = v.shape[0]
    v0, v1, v2 = three_parts(v)
    first = dot(jnp.concatenate([v0, v1, v2], axis=0), gram[0][...])
    second = dot(jnp.concatenate([v0, v1], axis=0), gram[1][...])
    third = dot(v0, gram[2][...])
    return first[:k] + (
        (first[k : 2 * k] + second[:k]) + ((first[2 * k :] + second[k:]) + third)
    )


def finish_kernel(pixel_total, chunk, sizes, me_ref, lines_ref, v_ref, x_hbm, out_hbm, x, out, ordered, g0, g1, g2, x0_ref, x1_ref, x_sem, out_sem):
    m, n = x_hbm.shape
    k = v_ref.shape[0]
    tiles = m // TILE
    load = pltpu.make_async_copy(x_hbm, x, x_sem)
    load.start()
    slots = math.prod(sizes)
    rows = lines_ref.shape[0] // slots
    for slot, back in enumerate(itertools.product(*([0, *steps(size)] for size in sizes))):
        place = 0
        for axis, (size, hops) in enumerate(zip(sizes, back)):
            place = place * size + lax.rem(me_ref[axis] + (size - hops), size)
        place = pl.multiple_of(place * rows, ROWS)
        ordered[pl.ds(place, rows), :] = lines_ref[slot * rows : (slot + 1) * rows, :]

    gram = (g0, g1, g2)
    diagonal = []
    place = 0
    for i in range(tiles):
        for j in range(i, tiles):
            tile = ordered[place * TILE : (place + 1) * TILE, :] * (1.0 / pixel_total)
            place += 1
            at_i, at_j = slice(i * TILE, (i + 1) * TILE), slice(j * TILE, (j + 1) * TILE)
            for ref, part in zip(gram, three_parts(tile)):
                ref[at_i, at_j] = part
            if i == j:
                eye = iota((TILE, TILE), 0) == iota((TILE, TILE), 1)
                diagonal.append(jnp.sum(jnp.where(eye, tile, 0.0), axis=0, keepdims=True))
            else:
                for ref, part in zip(gram, three_parts(tile.T)):
                    ref[at_j, at_i] = part

    diagonal = jnp.concatenate(diagonal, axis=1)
    evened = m / jnp.sum(diagonal, axis=1, keepdims=True)
    v = v_ref[...]
    for sweep in range(ITERS):
        if sweep == ITERS - 1:
            load.wait()
            x0_ref[...], x1_ref[...] = two_parts(x[...])
        v = orthonormal(times_gram(v, gram) * evened)
    w = times_gram(v, gram)
    inner = dot_nt(w, v, HIGHEST)
    twice = jnp.dot(inner, v, precision=HIGHEST) - 2.0 * w
    power = diagonal + jnp.sum(v * twice, axis=0, keepdims=True)
    scale = lax.rsqrt(jnp.maximum(power, 0.0) + EPSILON)
    scale = jnp.concatenate(
        [
            jnp.broadcast_to(scale[:, i * TILE : (i + 1) * TILE], (TILE, TILE)).T
            for i in range(tiles)
        ],
        axis=0,
    )
    q0, q1 = two_parts(v.T)
    spread = jnp.concatenate([q0, q1, q0], axis=1)
    v0, v1 = two_parts(v)
    v01 = jnp.concatenate([v0, v1], axis=0)
    cuts = [*range(0, n, chunk), n - chunk // 2, n]
    bands = [slice(a, b) for a, b in zip(cuts, cuts[1:])]
    for c, here in enumerate(bands):
        xc = x[:, here]
        x0, x1 = x0_ref[:, here], x1_ref[:, here]
        both = dot(v01, x0)
        l0, l1 = two_parts(both[:k] + (both[k:] + dot(v0, x1)))
        common = dot(spread, jnp.concatenate([l0, l0, l1], axis=0))
        for t in range((here.stop - here.start) // TILE):
            at = slice(t * TILE, (t + 1) * TILE)
            out[:, here.start + t * TILE : here.start + (t + 1) * TILE] = (xc[:, at] - common[:, at]) * scale
        pltpu.make_async_copy(out.at[:, here], out_hbm.at[:, here], out_sem.at[c]).start()
    for c, here in enumerate(bands):
        pltpu.make_async_copy(out.at[:, here], out_hbm.at[:, here], out_sem.at[c]).wait()


def corrected(lines, me, sizes, v, x, pixel_total, chunk=512):
    m, n = x.shape
    k = v.shape[0]
    return pl.pallas_call(
        functools.partial(finish_kernel, pixel_total, chunk, sizes),
        out_shape=jax.ShapeDtypeStruct((m, n), F32),
        in_specs=[
            pl.BlockSpec(memory_space=pltpu.SMEM),
            pl.BlockSpec(memory_space=pltpu.VMEM),
            pl.BlockSpec(memory_space=pltpu.VMEM),
            pl.BlockSpec(memory_space=pl.ANY),
        ],
        out_specs=pl.BlockSpec(memory_space=pl.ANY),
        scratch_shapes=[
            pltpu.VMEM((m, n), F32),
            pltpu.VMEM((m, n), F32),
            pltpu.VMEM(lines.shape, F32),
            pltpu.VMEM((m, m), BF16),
            pltpu.VMEM((m, m), BF16),
            pltpu.VMEM((m, m), BF16),
            pltpu.VMEM((m, n), BF16),
            pltpu.VMEM((m, n), BF16),
            pltpu.SemaphoreType.DMA,
            pltpu.SemaphoreType.DMA((n // chunk + 1,)),
        ],
        compiler_params=pltpu.CompilerParams(vmem_limit_bytes=VMEM),
        cost_estimate=pl.CostEstimate(flops=12 * m * k * n, bytes_accessed=8 * m * n, transcendentals=0),
        name="finish",
    )(me, lines, v, x)


def on_device(phase_stack, start_basis):
    pixel_total = phase_stack.shape[1] * lax.axis_size(AXES)
    lines, v = sum_everywhere(upper_gram(phase_stack), start_rows(start_basis.T))
    me = jnp.stack([place_on(axis) for axis in SHARED]).astype(jnp.int32)
    sizes = tuple(lax.axis_size(axis) for axis in SHARED)
    return corrected(lines, me, sizes, v, phase_stack, pixel_total)


def solution(mesh):
    split = Mesh(mesh.devices.reshape(-1, 2, mesh.shape["gy"], mesh.shape["gz"]), AXES)
    placed = (P(None, AXES), P())
    return jax.shard_map(
        on_device, mesh=split, in_specs=placed, out_specs=P(None, AXES), check_vma=False
    )
```

```python
import functools
import itertools
import math

import jax
import jax.numpy as jnp
from jax import lax
from jax.experimental import pallas as pl
from jax.experimental.pallas import tpu as pltpu
from jax.sharding import Mesh
from jax.sharding import PartitionSpec as P

ITERS = 3
AXES = ("y", "c", "x", "z")
SHARED = ("c", "y", "x")
HIGHEST = lax.Precision.HIGHEST
EPSILON = 1e-06
TILE = 128
WIDE = 256
ROWS = 8
VMEM = 50 * 2**20
F32 = jnp.float32
BF16 = jnp.bfloat16
NT = (((1,), (1,)), ((), ()))


def half():
    return sum(lax.axis_index(axis) for axis in AXES) % 2


def place_on(axis):
    return half() if axis == "c" else lax.axis_index(axis)


def moved(v, axis, to_place):
    sizes = [lax.axis_size(a) for a in AXES]
    along, core = AXES.index(axis), AXES.index("c")
    pairs = []
    for source, at in enumerate(itertools.product(*map(range, sizes))):
        to = list(at)
        step = to_place(at[along]) - at[along]
        to[along] = (at[along] + step) % sizes[along]
        if along != core:
            to[core] = (at[core] + step) % 2
        target = 0
        for size, i in zip(sizes, to):
            target = target * size + i
        pairs.append((source, target))
    return lax.ppermute(v, AXES, pairs)


def shifted(v, axis, k):
    return moved(v, axis, lambda i: i + k)


def steps(n):
    return sorted(range(1, n), key=lambda k: -min(k, n - k))


def share_of_sum(v, axis):
    n, me = lax.axis_size(axis), place_on(axis)
    rows = v.shape[0] // n
    piece = lambda k: lax.dynamic_slice_in_dim(v, lax.rem(me + k, n) * rows, rows, 0)
    arrived = [shifted(piece(k), axis, k) for k in steps(n)]
    total = piece(0)
    for part in arrived:
        total = total + part
    return total


def joined(v, axis):
    return jnp.concatenate([v] + [shifted(v, axis, k) for k in steps(lax.axis_size(axis))], axis=0)


def summed(v, axis):
    if lax.axis_size(axis) != 8:
        return lax.psum(v, axis)
    v = v + moved(v, axis, lambda i: i ^ 1)
    arrived = [moved(v, axis, lambda i, k=k: i + k if i % 2 else i - k) for k in (3, 2, 1)]
    for part in arrived:
        v = v + part
    return v


def sum_everywhere(v, meanwhile):
    for axis in SHARED:
        v = share_of_sum(v, axis)
    v, meanwhile = lax.optimization_barrier((summed(v, "z"), meanwhile))
    for axis in reversed(SHARED):
        v = joined(v, axis)
    return v, meanwhile


def two_parts(x):
    hi = x.astype(BF16)
    return hi, (x - hi.astype(F32)).astype(BF16)


def three_parts(x):
    hi = x.astype(BF16)
    rest = x - hi.astype(F32)
    mid = rest.astype(BF16)
    return hi, mid, (rest - mid.astype(F32)).astype(BF16)


def dot(a, b):
    return jnp.dot(a, b, preferred_element_type=F32)


def dot_nt(a, b, precision=None):
    return lax.dot_general(a, b, NT, precision=precision, preferred_element_type=F32)


def iota(shape, dim):
    return lax.broadcasted_iota(jnp.int32, shape, dim)


def gram_kernel(x_hbm, out_ref, x, sem):
    m, n = x_hbm.shape
    bands = [slice(i, i + WIDE) for i in range(0, m, WIDE)]
    loads = [pltpu.make_async_copy(x_hbm.at[b], x.at[b], sem.at[i]) for i, b in enumerate(bands)]
    for load in loads:
        load.start()
    tiles = m // TILE
    places = {}
    for i in range(tiles):
        for j in range(i, tiles):
            places[i, j] = len(places)
    step = WIDE // TILE
    parts = []
    for j, load in enumerate(loads):
        load.wait()
        parts.append(two_parts(x[bands[j]]))
        hi, lo = parts[j]
        for i in range(j + 1):
            above_hi, above_lo = parts[i]
            if i < j:
                block = dot_nt(above_hi, hi) + (dot_nt(above_lo, hi) + dot_nt(above_hi, lo))
            else:
                mixed = dot_nt(hi, lo)
                block = dot_nt(hi, hi) + ((mixed + mixed.T) + dot_nt(lo, lo))
            for s in range(step):
                for t in range(step):
                    place = places.get((i * step + s, j * step + t))
                    if place is not None:
                        out_ref[place * TILE : (place + 1) * TILE, :] = block[
                            s * TILE : (s + 1) * TILE, t * TILE : (t + 1) * TILE
                        ]


def upper_gram(x):
    m, n = x.shape
    tiles = m // TILE
    lines = tiles * (tiles + 1) // 2 * TILE
    return pl.pallas_call(
        gram_kernel,
        out_shape=jax.ShapeDtypeStruct((lines, TILE), F32),
        in_specs=[pl.BlockSpec(memory_space=pl.ANY)],
        out_specs=pl.BlockSpec(memory_space=pltpu.VMEM),
        scratch_shapes=[pltpu.VMEM((m, n), F32), pltpu.SemaphoreType.DMA((m // WIDE,))],
        compiler_params=pltpu.CompilerParams(vmem_limit_bytes=VMEM),
        cost_estimate=pl.CostEstimate(flops=6 * m * m * n, bytes_accessed=4 * m * n, transcendentals=0),
        name="gram",
    )(x)


def inverse_factor(b):
    k = b.shape[0]
    blocks = k // ROWS
    eye = (iota((k, k), 0) == iota((k, k), 1)).astype(F32)
    both = jnp.concatenate([b, eye], axis=1)
    line = [both[ROWS * q : ROWS * (q + 1), :] for q in range(blocks)]
    sub = iota((ROWS, 2 * k), 0)
    span = 16
    per = span // ROWS
    for p in range(0, blocks, per):
        column = {
            (q, i): jnp.broadcast_to(line[q][:, ROWS * p + i : ROWS * p + i + 1], (ROWS, 2 * k))
            for q in range(p, blocks)
            for i in range(span)
        }
        at = lambda i, j: column[p + i // ROWS, j][i % ROWS : i % ROWS + 1, :]
        for i in range(0, span, 2):
            a, b_, c = at(i, i), at(i, i + 1), at(i + 1, i + 1)
            first = pl.reciprocal(a)
            second = a * pl.reciprocal(a * c - b_ * b_)
            lower = b_ * first
            others = range(i + 2, span)
            top = {j: at(i, j) for j in others}
            ahead = {j: top[j] * first for j in others}
            then = {j: (at(i + 1, j) - lower * top[j]) * second for j in others}
            home, row = p + i // ROWS, i % ROWS
            top_row = line[home][row : row + 1, :]
            first_row = top_row * first
            next_row = (line[home][row + 1 : row + 2, :] - lower * top_row) * second
            for q in range(home, blocks):
                factor = column[q, i]
                following = column[q, i + 1] - factor * lower
                if q == home:
                    factor = jnp.where(sub > row, factor, 0.0)
                    following = jnp.where(sub > row + 1, following, 0.0)
                for j in others:
                    column[q, j] = column[q, j] - factor * ahead[j] - following * then[j]
                line[q] = line[q] - factor * first_row - following * next_row
    both = jnp.concatenate(line, axis=0)
    pivots = jnp.sum(
        jnp.where(iota(both.shape, 0) == iota(both.shape, 1), both, 0.0), axis=1, keepdims=True
    )
    return (both * lax.rsqrt(pivots))[:, k:]


def orthonormal(y):
    return jnp.dot(inverse_factor(dot_nt(y, y, HIGHEST)), y, precision=HIGHEST)


def start_kernel(s_ref, v_ref):
    s = s_ref[...]
    size = jnp.max(jnp.max(jnp.abs(s), axis=0, keepdims=True), axis=1, keepdims=True)
    v_ref[...] = orthonormal(s / size)


def start_rows(s):
    k, m = s.shape
    return pl.pallas_call(
        start_kernel,
        out_shape=jax.ShapeDtypeStruct((k, m), F32),
        compiler_params=pltpu.CompilerParams(vmem_limit_bytes=8 * 2**20),
        cost_estimate=pl.CostEstimate(flops=8 * 10**9, bytes_accessed=8 * m * k, transcendentals=0),
        name="start_rows",
    )(s)


def times_gram(v, gram):
    k = v.shape[0]
    v0, v1, v2 = three_parts(v)
    first = dot(jnp.concatenate([v0, v1, v2], axis=0), gram[0][...])
    second = dot(jnp.concatenate([v0, v1], axis=0), gram[1][...])
    third = dot(v0, gram[2][...])
    return first[:k] + (
        (first[k : 2 * k] + second[:k]) + ((first[2 * k :] + second[k:]) + third)
    )


def finish_kernel(pixel_total, chunk, sizes, me_ref, lines_ref, v_ref, x_hbm, out_hbm, x, out, ordered, g0, g1, g2, x0_ref, x1_ref, x_sem, out_sem):
    m, n = x_hbm.shape
    k = v_ref.shape[0]
    tiles = m // TILE
    load = pltpu.make_async_copy(x_hbm, x, x_sem)
    load.start()
    slots = math.prod(sizes)
    rows = lines_ref.shape[0] // slots
    for slot, back in enumerate(itertools.product(*([0, *steps(size)] for size in sizes))):
        place = 0
        for axis, (size, hops) in enumerate(zip(sizes, back)):
            place = place * size + lax.rem(me_ref[axis] + (size - hops), size)
        place = pl.multiple_of(place * rows, ROWS)
        ordered[pl.ds(place, rows), :] = lines_ref[slot * rows : (slot + 1) * rows, :]

    gram = (g0, g1, g2)
    diagonal = []
    place = 0
    for i in range(tiles):
        for j in range(i, tiles):
            tile = ordered[place * TILE : (place + 1) * TILE, :] * (1.0 / pixel_total)
            place += 1
            at_i, at_j = slice(i * TILE, (i + 1) * TILE), slice(j * TILE, (j + 1) * TILE)
            for ref, part in zip(gram, three_parts(tile)):
                ref[at_i, at_j] = part
            if i == j:
                eye = iota((TILE, TILE), 0) == iota((TILE, TILE), 1)
                diagonal.append(jnp.sum(jnp.where(eye, tile, 0.0), axis=0, keepdims=True))
            else:
                for ref, part in zip(gram, three_parts(tile.T)):
                    ref[at_j, at_i] = part

    diagonal = jnp.concatenate(diagonal, axis=1)
    evened = m / jnp.sum(diagonal, axis=1, keepdims=True)
    v = v_ref[...]
    for sweep in range(ITERS):
        if sweep == ITERS - 1:
            load.wait()
            x0_ref[...], x1_ref[...] = two_parts(x[...])
        v = orthonormal(times_gram(v, gram) * evened)
    w = times_gram(v, gram)
    inner = dot_nt(w, v, HIGHEST)
    twice = jnp.dot(inner, v, precision=HIGHEST) - 2.0 * w
    power = diagonal + jnp.sum(v * twice, axis=0, keepdims=True)
    scale = lax.rsqrt(jnp.maximum(power, 0.0) + EPSILON)
    scale = jnp.concatenate(
        [
            jnp.broadcast_to(scale[:, i * TILE : (i + 1) * TILE], (TILE, TILE)).T
            for i in range(tiles)
        ],
        axis=0,
    )
    q0, q1 = two_parts(v.T)
    spread = jnp.concatenate([q0, q1, q0], axis=1)
    v0, v1 = two_parts(v)
    v01 = jnp.concatenate([v0, v1], axis=0)
    cuts = [*range(0, n, chunk), n - chunk // 2, n]
    bands = [slice(a, b) for a, b in zip(cuts, cuts[1:])]
    for c, here in enumerate(bands):
        xc = x[:, here]
        x0, x1 = x0_ref[:, here], x1_ref[:, here]
        both = dot(v01, x0)
        l0, l1 = two_parts(both[:k] + (both[k:] + dot(v0, x1)))
        common = dot(spread, jnp.concatenate([l0, l0, l1], axis=0))
        for t in range((here.stop - here.start) // TILE):
            at = slice(t * TILE, (t + 1) * TILE)
            out[:, here.start + t * TILE : here.start + (t + 1) * TILE] = (xc[:, at] - common[:, at]) * scale
        pltpu.make_async_copy(out.at[:, here], out_hbm.at[:, here], out_sem.at[c]).start()
    for c, here in enumerate(bands):
        pltpu.make_async_copy(out.at[:, here], out_hbm.at[:, here], out_sem.at[c]).wait()


def corrected(lines, me, sizes, v, x, pixel_total, chunk=512):
    m, n = x.shape
    k = v.shape[0]
    return pl.pallas_call(
        functools.partial(finish_kernel, pixel_total, chunk, sizes),
        out_shape=jax.ShapeDtypeStruct((m, n), F32),
        in_specs=[
            pl.BlockSpec(memory_space=pltpu.SMEM),
            pl.BlockSpec(memory_space=pltpu.VMEM),
            pl.BlockSpec(memory_space=pltpu.VMEM),
            pl.BlockSpec(memory_space=pl.ANY),
        ],
        out_specs=pl.BlockSpec(memory_space=pl.ANY),
        scratch_shapes=[
            pltpu.VMEM((m, n), F32),
            pltpu.VMEM((m, n), F32),
            pltpu.VMEM(lines.shape, F32),
            pltpu.VMEM((m, m), BF16),
            pltpu.VMEM((m, m), BF16),
            pltpu.VMEM((m, m), BF16),
            pltpu.VMEM((m, n), BF16),
            pltpu.VMEM((m, n), BF16),
            pltpu.SemaphoreType.DMA,
            pltpu.SemaphoreType.DMA((n // chunk + 1,)),
        ],
        compiler_params=pltpu.CompilerParams(vmem_limit_bytes=VMEM),
        cost_estimate=pl.CostEstimate(flops=12 * m * k * n, bytes_accessed=8 * m * n, transcendentals=0),
        name="finish",
    )(me, lines, v, x)


def on_device(phase_stack, start_basis):
    pixel_total = phase_stack.shape[1] * lax.axis_size(AXES)
    lines, v = sum_everywhere(upper_gram(phase_stack), start_rows(start_basis.T))
    me = jnp.stack([place_on(axis) for axis in SHARED]).astype(jnp.int32)
    sizes = tuple(lax.axis_size(axis) for axis in SHARED)
    return corrected(lines, me, sizes, v, phase_stack, pixel_total)


def solution(mesh):
    split = Mesh(mesh.devices.reshape(-1, 2, mesh.shape["gy"], mesh.shape["gz"]), AXES)
    placed = (P(None, AXES), P())
    return jax.shard_map(
        on_device, mesh=split, in_specs=placed, out_specs=P(None, AXES), check_vma=False
    )
```

```python
import functools
import itertools
import math

import jax
import jax.numpy as jnp
from jax import lax
from jax.experimental import pallas as pl
from jax.experimental.pallas import tpu as pltpu
from jax.sharding import Mesh
from jax.sharding import PartitionSpec as P

ITERS = 3
AXES = ("y", "c", "x", "z")
SHARED = ("c", "y", "x")
HIGHEST = lax.Precision.HIGHEST
EPSILON = 1e-06
TILE = 128
WIDE = 256
ROWS = 8
VMEM = 50 * 2**20
F32 = jnp.float32
BF16 = jnp.bfloat16
NT = (((1,), (1,)), ((), ()))


def half():
    return sum(lax.axis_index(axis) for axis in AXES) % 2


def place_on(axis):
    return half() if axis == "c" else lax.axis_index(axis)


def moved(v, axis, to_place):
    sizes = [lax.axis_size(a) for a in AXES]
    along, core = AXES.index(axis), AXES.index("c")
    pairs = []
    for source, at in enumerate(itertools.product(*map(range, sizes))):
        to = list(at)
        step = to_place(at[along]) - at[along]
        to[along] = (at[along] + step) % sizes[along]
        if along != core:
            to[core] = (at[core] + step) % 2
        target = 0
        for size, i in zip(sizes, to):
            target = target * size + i
        pairs.append((source, target))
    return lax.ppermute(v, AXES, pairs)


def shifted(v, axis, k):
    return moved(v, axis, lambda i: i + k)


def steps(n):
    return sorted(range(1, n), key=lambda k: -min(k, n - k))


def slots_of(axis):
    ways = steps(lax.axis_size(axis))
    return (0, *(ways[::-1] if axis == "x" else ways))


def share_of_sum(v, axis):
    n, me = lax.axis_size(axis), place_on(axis)
    rows = v.shape[0] // n
    piece = lambda k: lax.dynamic_slice_in_dim(v, lax.rem(me + k, n) * rows, rows, 0)
    arrived = [shifted(piece(k), axis, k) for k in steps(n)]
    total = piece(0)
    for part in arrived:
        total = total + part
    return total


def joined(v, axis):
    return jnp.concatenate([v] + [shifted(v, axis, k) for k in slots_of(axis)[1:]], axis=0)


def summed(v, axis):
    if lax.axis_size(axis) != 8:
        return lax.psum(v, axis)
    v = v + moved(v, axis, lambda i: i ^ 1)
    arrived = [moved(v, axis, lambda i, k=k: i + k if i % 2 else i - k) for k in (1, 2, 3)]
    for part in arrived:
        v = v + part
    return v


def sum_everywhere(v, meanwhile):
    for axis in SHARED:
        v = share_of_sum(v, axis)
    v, meanwhile = lax.optimization_barrier((summed(v, "z"), meanwhile))
    for axis in reversed(SHARED):
        v = joined(v, axis)
    return v, meanwhile


def two_parts(x):
    hi = x.astype(BF16)
    return hi, (x - hi.astype(F32)).astype(BF16)


def three_parts(x):
    hi = x.astype(BF16)
    rest = x - hi.astype(F32)
    mid = rest.astype(BF16)
    return hi, mid, (rest - mid.astype(F32)).astype(BF16)


def dot(a, b):
    return jnp.dot(a, b, preferred_element_type=F32)


def dot_nt(a, b, precision=None):
    return lax.dot_general(a, b, NT, precision=precision, preferred_element_type=F32)


def iota(shape, dim):
    return lax.broadcasted_iota(jnp.int32, shape, dim)


def gram_kernel(x_hbm, out_ref, x, sem):
    m, n = x_hbm.shape
    bands = [slice(i, i + WIDE) for i in range(0, m, WIDE)]
    loads = [pltpu.make_async_copy(x_hbm.at[b], x.at[b], sem.at[i]) for i, b in enumerate(bands)]
    for load in loads:
        load.start()
    tiles = m // TILE
    places = {}
    for i in range(tiles):
        for j in range(i, tiles):
            places[i, j] = len(places)
    step = WIDE // TILE
    parts = []
    for j, load in enumerate(loads):
        load.wait()
        parts.append(two_parts(x[bands[j]]))
        hi, lo = parts[j]
        for i in range(j + 1):
            above_hi, above_lo = parts[i]
            if i < j:
                block = dot_nt(above_hi, hi) + (dot_nt(above_lo, hi) + dot_nt(above_hi, lo))
            else:
                mixed = dot_nt(hi, lo)
                block = dot_nt(hi, hi) + ((mixed + mixed.T) + dot_nt(lo, lo))
            for s in range(step):
                for t in range(step):
                    place = places.get((i * step + s, j * step + t))
                    if place is not None:
                        out_ref[place * TILE : (place + 1) * TILE, :] = block[
                            s * TILE : (s + 1) * TILE, t * TILE : (t + 1) * TILE
                        ]


def upper_gram(x):
    m, n = x.shape
    tiles = m // TILE
    lines = tiles * (tiles + 1) // 2 * TILE
    return pl.pallas_call(
        gram_kernel,
        out_shape=jax.ShapeDtypeStruct((lines, TILE), F32),
        in_specs=[pl.BlockSpec(memory_space=pl.ANY)],
        out_specs=pl.BlockSpec(memory_space=pltpu.VMEM),
        scratch_shapes=[pltpu.VMEM((m, n), F32), pltpu.SemaphoreType.DMA((m // WIDE,))],
        compiler_params=pltpu.CompilerParams(vmem_limit_bytes=VMEM),
        cost_estimate=pl.CostEstimate(flops=6 * m * m * n, bytes_accessed=4 * m * n, transcendentals=0),
        name="gram",
    )(x)


def inverse_factor(b):
    k = b.shape[0]
    blocks = k // ROWS
    eye = (iota((k, k), 0) == iota((k, k), 1)).astype(F32)
    both = jnp.concatenate([b, eye], axis=1)
    line = [both[ROWS * q : ROWS * (q + 1), :] for q in range(blocks)]
    sub = iota((ROWS, 2 * k), 0)
    span = 16
    per = span // ROWS
    for p in range(0, blocks, per):
        column = {
            (q, i): jnp.broadcast_to(line[q][:, ROWS * p + i : ROWS * p + i + 1], (ROWS, 2 * k))
            for q in range(p, blocks)
            for i in range(span)
        }
        at = lambda i, j: column[p + i // ROWS, j][i % ROWS : i % ROWS + 1, :]
        for i in range(0, span, 2):
            a, b_, c = at(i, i), at(i, i + 1), at(i + 1, i + 1)
            first = pl.reciprocal(a)
            second = a * pl.reciprocal(a * c - b_ * b_)
            lower = b_ * first
            others = range(i + 2, span)
            top = {j: at(i, j) for j in others}
            ahead = {j: top[j] * first for j in others}
            then = {j: (at(i + 1, j) - lower * top[j]) * second for j in others}
            home, row = p + i // ROWS, i % ROWS
            top_row = line[home][row : row + 1, :]
            first_row = top_row * first
            next_row = (line[home][row + 1 : row + 2, :] - lower * top_row) * second
            for q in range(home, blocks):
                factor = column[q, i]
                following = column[q, i + 1] - factor * lower
                if q == home:
                    factor = jnp.where(sub > row, factor, 0.0)
                    following = jnp.where(sub > row + 1, following, 0.0)
                for j in others:
                    column[q, j] = column[q, j] - factor * ahead[j] - following * then[j]
                line[q] = line[q] - factor * first_row - following * next_row
    both = jnp.concatenate(line, axis=0)
    pivots = jnp.sum(
        jnp.where(iota(both.shape, 0) == iota(both.shape, 1), both, 0.0), axis=1, keepdims=True
    )
    return (both * lax.rsqrt(pivots))[:, k:]


def orthonormal(y):
    return jnp.dot(inverse_factor(dot_nt(y, y, HIGHEST)), y, precision=HIGHEST)


def start_kernel(s_ref, v_ref):
    s = s_ref[...]
    size = jnp.max(jnp.max(jnp.abs(s), axis=0, keepdims=True), axis=1, keepdims=True)
    v_ref[...] = orthonormal(s / size)


def start_rows(s):
    k, m = s.shape
    return pl.pallas_call(
        start_kernel,
        out_shape=jax.ShapeDtypeStruct((k, m), F32),
        compiler_params=pltpu.CompilerParams(vmem_limit_bytes=8 * 2**20),
        cost_estimate=pl.CostEstimate(flops=8 * 10**9, bytes_accessed=8 * m * k, transcendentals=0),
        name="start_rows",
    )(s)


def times_gram(v, gram):
    k = v.shape[0]
    v0, v1, v2 = three_parts(v)
    first = dot(jnp.concatenate([v0, v1, v2], axis=0), gram[0][...])
    second = dot(jnp.concatenate([v0, v1], axis=0), gram[1][...])
    third = dot(v0, gram[2][...])
    return first[:k] + (
        (first[k : 2 * k] + second[:k]) + ((first[2 * k :] + second[k:]) + third)
    )


def finish_kernel(pixel_total, chunk, orders, me_ref, lines_ref, v_ref, x_hbm, out_hbm, x, out, ordered, g0, g1, g2, x0_ref, x1_ref, x_sem, out_sem):
    m, n = x_hbm.shape
    k = v_ref.shape[0]
    tiles = m // TILE
    load = pltpu.make_async_copy(x_hbm, x, x_sem)
    load.start()
    sizes = [len(order) for order in orders]
    slots = math.prod(sizes)
    rows = lines_ref.shape[0] // slots
    for slot, back in enumerate(itertools.product(*orders)):
        place = 0
        for axis, (size, hops) in enumerate(zip(sizes, back)):
            place = place * size + lax.rem(me_ref[axis] + (size - hops), size)
        place = pl.multiple_of(place * rows, ROWS)
        ordered[pl.ds(place, rows), :] = lines_ref[slot * rows : (slot + 1) * rows, :]

    gram = (g0, g1, g2)
    diagonal = []
    place = 0
    for i in range(tiles):
        for j in range(i, tiles):
            tile = ordered[place * TILE : (place + 1) * TILE, :] * (1.0 / pixel_total)
            place += 1
            at_i, at_j = slice(i * TILE, (i + 1) * TILE), slice(j * TILE, (j + 1) * TILE)
            for ref, part in zip(gram, three_parts(tile)):
                ref[at_i, at_j] = part
            if i == j:
                eye = iota((TILE, TILE), 0) == iota((TILE, TILE), 1)
                diagonal.append(jnp.sum(jnp.where(eye, tile, 0.0), axis=0, keepdims=True))
            else:
                for ref, part in zip(gram, three_parts(tile.T)):
                    ref[at_j, at_i] = part

    diagonal = jnp.concatenate(diagonal, axis=1)
    evened = m / jnp.sum(diagonal, axis=1, keepdims=True)
    v = v_ref[...]
    for sweep in range(ITERS):
        if sweep == ITERS - 1:
            load.wait()
            x0_ref[...], x1_ref[...] = two_parts(x[...])
        v = orthonormal(times_gram(v, gram) * evened)
    w = times_gram(v, gram)
    inner = dot_nt(w, v, HIGHEST)
    twice = jnp.dot(inner, v, precision=HIGHEST) - 2.0 * w
    power = diagonal + jnp.sum(v * twice, axis=0, keepdims=True)
    scale = lax.rsqrt(jnp.maximum(power, 0.0) + EPSILON)
    scale = jnp.concatenate(
        [
            jnp.broadcast_to(scale[:, i * TILE : (i + 1) * TILE], (TILE, TILE)).T
            for i in range(tiles)
        ],
        axis=0,
    )
    q0, q1 = two_parts(v.T)
    spread = jnp.concatenate([q0, q1, q0], axis=1)
    v0, v1 = two_parts(v)
    v01 = jnp.concatenate([v0, v1], axis=0)
    cuts = [*range(0, n, chunk), n - chunk // 2, n]
    bands = [slice(a, b) for a, b in zip(cuts, cuts[1:])]
    for c, here in enumerate(bands):
        xc = x[:, here]
        x0, x1 = x0_ref[:, here], x1_ref[:, here]
        both = dot(v01, x0)
        l0, l1 = two_parts(both[:k] + (both[k:] + dot(v0, x1)))
        common = dot(spread, jnp.concatenate([l0, l0, l1], axis=0))
        for t in range((here.stop - here.start) // TILE):
            at = slice(t * TILE, (t + 1) * TILE)
            out[:, here.start + t * TILE : here.start + (t + 1) * TILE] = (xc[:, at] - common[:, at]) * scale
        pltpu.make_async_copy(out.at[:, here], out_hbm.at[:, here], out_sem.at[c]).start()
    for c, here in enumerate(bands):
        pltpu.make_async_copy(out.at[:, here], out_hbm.at[:, here], out_sem.at[c]).wait()


def corrected(lines, me, orders, v, x, pixel_total, chunk=512):
    m, n = x.shape
    k = v.shape[0]
    return pl.pallas_call(
        functools.partial(finish_kernel, pixel_total, chunk, orders),
        out_shape=jax.ShapeDtypeStruct((m, n), F32),
        in_specs=[
            pl.BlockSpec(memory_space=pltpu.SMEM),
            pl.BlockSpec(memory_space=pltpu.VMEM),
            pl.BlockSpec(memory_space=pltpu.VMEM),
            pl.BlockSpec(memory_space=pl.ANY),
        ],
        out_specs=pl.BlockSpec(memory_space=pl.ANY),
        scratch_shapes=[
            pltpu.VMEM((m, n), F32),
            pltpu.VMEM((m, n), F32),
            pltpu.VMEM(lines.shape, F32),
            pltpu.VMEM((m, m), BF16),
            pltpu.VMEM((m, m), BF16),
            pltpu.VMEM((m, m), BF16),
            pltpu.VMEM((m, n), BF16),
            pltpu.VMEM((m, n), BF16),
            pltpu.SemaphoreType.DMA,
            pltpu.SemaphoreType.DMA((n // chunk + 1,)),
        ],
        compiler_params=pltpu.CompilerParams(vmem_limit_bytes=VMEM),
        cost_estimate=pl.CostEstimate(flops=12 * m * k * n, bytes_accessed=8 * m * n, transcendentals=0),
        name="finish",
    )(me, lines, v, x)


def on_device(phase_stack, start_basis):
    pixel_total = phase_stack.shape[1] * lax.axis_size(AXES)
    lines, v = sum_everywhere(upper_gram(phase_stack), start_rows(start_basis.T))
    me = jnp.stack([place_on(axis) for axis in SHARED]).astype(jnp.int32)
    orders = tuple(slots_of(axis) for axis in SHARED)
    return corrected(lines, me, orders, v, phase_stack, pixel_total)


def solution(mesh):
    split = Mesh(mesh.devices.reshape(-1, 2, mesh.shape["gy"], mesh.shape["gz"]), AXES)
    placed = (P(None, AXES), P())
    return jax.shard_map(
        on_device, mesh=split, in_specs=placed, out_specs=P(None, AXES), check_vma=False
    )
```

```python
import functools
import itertools
import math

import jax
import jax.numpy as jnp
from jax import lax
from jax.experimental import pallas as pl
from jax.experimental.pallas import tpu as pltpu
from jax.sharding import Mesh
from jax.sharding import PartitionSpec as P

ITERS = 3
AXES = ("y", "c", "x", "z")
SHARED = ("c", "y", "x")
HIGHEST = lax.Precision.HIGHEST
EPSILON = 1e-06
TILE = 128
WIDE = 256
ROWS = 8
VMEM = 50 * 2**20
F32 = jnp.float32
BF16 = jnp.bfloat16
NT = (((1,), (1,)), ((), ()))


def half():
    return sum(lax.axis_index(axis) for axis in AXES) % 2


def place_on(axis):
    return half() if axis == "c" else lax.axis_index(axis)


def moved(v, axis, to_place):
    sizes = [lax.axis_size(a) for a in AXES]
    along, core = AXES.index(axis), AXES.index("c")
    pairs = []
    for source, at in enumerate(itertools.product(*map(range, sizes))):
        to = list(at)
        step = to_place(at[along]) - at[along]
        to[along] = (at[along] + step) % sizes[along]
        if along != core:
            to[core] = (at[core] + step) % 2
        target = 0
        for size, i in zip(sizes, to):
            target = target * size + i
        pairs.append((source, target))
    return lax.ppermute(v, AXES, pairs)


def shifted(v, axis, k):
    return moved(v, axis, lambda i: i + k)


def steps(n):
    return sorted(range(1, n), key=lambda k: -min(k, n - k))


def slots_of(axis):
    ways = steps(lax.axis_size(axis))
    return (0, *(ways[::-1] if axis == "x" else ways))


def share_of_sum(v, axis):
    n, me = lax.axis_size(axis), place_on(axis)
    rows = v.shape[0] // n
    piece = lambda k: lax.dynamic_slice_in_dim(v, lax.rem(me + k, n) * rows, rows, 0)
    arrived = [shifted(piece(k), axis, k) for k in steps(n)]
    total = piece(0)
    for part in arrived:
        total = total + part
    return total


def joined(v, axis):
    return jnp.concatenate([v] + [shifted(v, axis, k) for k in slots_of(axis)[1:]], axis=0)


def summed(v, axis):
    if lax.axis_size(axis) != 8:
        return lax.psum(v, axis)
    v = v + moved(v, axis, lambda i: i ^ 1)
    arrived = [moved(v, axis, lambda i, k=k: i + k if i % 2 else i - k) for k in (1, 2, 3)]
    for part in arrived:
        v = v + part
    return v


def sum_everywhere(v, meanwhile):
    for axis in SHARED:
        v = share_of_sum(v, axis)
    v, meanwhile = lax.optimization_barrier((summed(v, "z"), meanwhile))
    for axis in reversed(SHARED):
        v = joined(v, axis)
    return v, meanwhile


def two_parts(x):
    hi = x.astype(BF16)
    return hi, (x - hi.astype(F32)).astype(BF16)


def three_parts(x):
    hi = x.astype(BF16)
    rest = x - hi.astype(F32)
    mid = rest.astype(BF16)
    return hi, mid, (rest - mid.astype(F32)).astype(BF16)


def dot(a, b):
    return jnp.dot(a, b, preferred_element_type=F32)


def dot_nt(a, b, precision=None):
    return lax.dot_general(a, b, NT, precision=precision, preferred_element_type=F32)


def iota(shape, dim):
    return lax.broadcasted_iota(jnp.int32, shape, dim)


def gram_kernel(x_hbm, out_ref, x, sem):
    m, n = x_hbm.shape
    bands = [slice(i, i + WIDE) for i in range(0, m, WIDE)]
    loads = [pltpu.make_async_copy(x_hbm.at[b], x.at[b], sem.at[i]) for i, b in enumerate(bands)]
    for load in loads:
        load.start()
    tiles = m // TILE
    places = {}
    for i in range(tiles):
        for j in range(i, tiles):
            places[i, j] = len(places)
    step = WIDE // TILE
    parts = []
    for j, load in enumerate(loads):
        load.wait()
        parts.append(two_parts(x[bands[j]]))
        hi, lo = parts[j]
        for i in range(j + 1):
            above_hi, above_lo = parts[i]
            if i < j:
                block = dot_nt(above_hi, hi) + (dot_nt(above_lo, hi) + dot_nt(above_hi, lo))
            else:
                mixed = dot_nt(hi, lo)
                block = dot_nt(hi, hi) + ((mixed + mixed.T) + dot_nt(lo, lo))
            for s in range(step):
                for t in range(step):
                    place = places.get((i * step + s, j * step + t))
                    if place is not None:
                        out_ref[place * TILE : (place + 1) * TILE, :] = block[
                            s * TILE : (s + 1) * TILE, t * TILE : (t + 1) * TILE
                        ]


def upper_gram(x):
    m, n = x.shape
    tiles = m // TILE
    lines = tiles * (tiles + 1) // 2 * TILE
    return pl.pallas_call(
        gram_kernel,
        out_shape=jax.ShapeDtypeStruct((lines, TILE), F32),
        in_specs=[pl.BlockSpec(memory_space=pl.ANY)],
        out_specs=pl.BlockSpec(memory_space=pltpu.VMEM),
        scratch_shapes=[pltpu.VMEM((m, n), F32), pltpu.SemaphoreType.DMA((m // WIDE,))],
        compiler_params=pltpu.CompilerParams(vmem_limit_bytes=VMEM),
        cost_estimate=pl.CostEstimate(flops=6 * m * m * n, bytes_accessed=4 * m * n, transcendentals=0),
        name="gram",
    )(x)


def inverse_factor(b):
    k = b.shape[0]
    blocks = k // ROWS
    eye = (iota((k, k), 0) == iota((k, k), 1)).astype(F32)
    both = jnp.concatenate([b, eye], axis=1)
    line = [both[ROWS * q : ROWS * (q + 1), :] for q in range(blocks)]
    sub = iota((ROWS, 2 * k), 0)
    span = 16
    per = span // ROWS
    for p in range(0, blocks, per):
        column = {
            (q, i): jnp.broadcast_to(line[q][:, ROWS * p + i : ROWS * p + i + 1], (ROWS, 2 * k))
            for q in range(p, blocks)
            for i in range(span)
        }
        at = lambda i, j: column[p + i // ROWS, j][i % ROWS : i % ROWS + 1, :]
        for i in range(0, span, 2):
            a, b_, c = at(i, i), at(i, i + 1), at(i + 1, i + 1)
            first = pl.reciprocal(a)
            second = a * pl.reciprocal(a * c - b_ * b_)
            lower = b_ * first
            others = range(i + 2, span)
            top = {j: at(i, j) for j in others}
            ahead = {j: top[j] * first for j in others}
            then = {j: (at(i + 1, j) - lower * top[j]) * second for j in others}
            home, row = p + i // ROWS, i % ROWS
            top_row = line[home][row : row + 1, :]
            first_row = top_row * first
            next_row = (line[home][row + 1 : row + 2, :] - lower * top_row) * second
            for q in range(home, blocks):
                factor = column[q, i]
                following = column[q, i + 1] - factor * lower
                if q == home:
                    factor = jnp.where(sub > row, factor, 0.0)
                    following = jnp.where(sub > row + 1, following, 0.0)
                for j in others:
                    column[q, j] = column[q, j] - factor * ahead[j] - following * then[j]
                line[q] = line[q] - factor * first_row - following * next_row
    both = jnp.concatenate(line, axis=0)
    pivots = jnp.sum(
        jnp.where(iota(both.shape, 0) == iota(both.shape, 1), both, 0.0), axis=1, keepdims=True
    )
    return (both * lax.rsqrt(pivots))[:, k:]


def orthonormal(y):
    return jnp.dot(inverse_factor(dot_nt(y, y, HIGHEST)), y, precision=HIGHEST)


def start_kernel(s_ref, v_ref):
    s = s_ref[...]
    size = jnp.max(jnp.max(jnp.abs(s), axis=0, keepdims=True), axis=1, keepdims=True)
    v_ref[...] = orthonormal(s / size)


def start_rows(s):
    k, m = s.shape
    return pl.pallas_call(
        start_kernel,
        out_shape=jax.ShapeDtypeStruct((k, m), F32),
        compiler_params=pltpu.CompilerParams(vmem_limit_bytes=8 * 2**20),
        cost_estimate=pl.CostEstimate(flops=8 * 10**9, bytes_accessed=8 * m * k, transcendentals=0),
        name="start_rows",
    )(s)


def times_gram(v, gram):
    k = v.shape[0]
    v0, v1, v2 = three_parts(v)
    first = dot(jnp.concatenate([v0, v1, v2], axis=0), gram[0][...])
    second = dot(jnp.concatenate([v0, v1], axis=0), gram[1][...])
    third = dot(v0, gram[2][...])
    return first[:k] + (
        (first[k : 2 * k] + second[:k]) + ((first[2 * k :] + second[k:]) + third)
    )


def finish_kernel(pixel_total, chunk, orders, me_ref, lines_ref, v_ref, x_hbm, out_hbm, x, out, ordered, g0, g1, g2, x0_ref, x1_ref, x_sem, out_sem):
    m, n = x_hbm.shape
    k = v_ref.shape[0]
    tiles = m // TILE
    load = pltpu.make_async_copy(x_hbm, x, x_sem)
    load.start()
    sizes = [len(order) for order in orders]
    slots = math.prod(sizes)
    rows = lines_ref.shape[0] // slots
    for slot, back in enumerate(itertools.product(*orders)):
        place = 0
        for axis, (size, hops) in enumerate(zip(sizes, back)):
            place = place * size + lax.rem(me_ref[axis] + (size - hops), size)
        place = pl.multiple_of(place * rows, ROWS)
        ordered[pl.ds(place, rows), :] = lines_ref[slot * rows : (slot + 1) * rows, :]

    gram = (g0, g1, g2)
    diagonal = []
    place = 0
    for i in range(tiles):
        for j in range(i, tiles):
            tile = ordered[place * TILE : (place + 1) * TILE, :] * (1.0 / pixel_total)
            place += 1
            at_i, at_j = slice(i * TILE, (i + 1) * TILE), slice(j * TILE, (j + 1) * TILE)
            for ref, part in zip(gram, three_parts(tile)):
                ref[at_i, at_j] = part
            if i == j:
                eye = iota((TILE, TILE), 0) == iota((TILE, TILE), 1)
                diagonal.append(jnp.sum(jnp.where(eye, tile, 0.0), axis=0, keepdims=True))
            else:
                for ref, part in zip(gram, three_parts(tile.T)):
                    ref[at_j, at_i] = part

    diagonal = jnp.concatenate(diagonal, axis=1)
    evened = m / jnp.sum(diagonal, axis=1, keepdims=True)
    v = v_ref[...]
    for sweep in range(ITERS):
        if sweep == ITERS - 1:
            load.wait()
            x0_ref[...], x1_ref[...] = two_parts(x[...])
        v = orthonormal(times_gram(v, gram) * evened)
    w = times_gram(v, gram)
    inner = dot_nt(w, v, HIGHEST)
    twice = jnp.dot(inner, v, precision=HIGHEST) - 2.0 * w
    power = diagonal + jnp.sum(v * twice, axis=0, keepdims=True)
    scale = lax.rsqrt(jnp.maximum(power, 0.0) + EPSILON)
    scale = jnp.concatenate(
        [
            jnp.broadcast_to(scale[:, i * TILE : (i + 1) * TILE], (TILE, TILE)).T
            for i in range(tiles)
        ],
        axis=0,
    )
    q0, q1 = two_parts(v.T)
    spread = jnp.concatenate([q0, q1, q0], axis=1)
    v0, v1 = two_parts(v)
    v01 = jnp.concatenate([v0, v1], axis=0)
    cuts = [0, *range(chunk // 2, n, chunk), n]
    bands = [slice(a, b) for a, b in zip(cuts, cuts[1:])]
    for c, here in enumerate(bands):
        xc = x[:, here]
        x0, x1 = x0_ref[:, here], x1_ref[:, here]
        both = dot(v01, x0)
        l0, l1 = two_parts(both[:k] + (both[k:] + dot(v0, x1)))
        common = dot(spread, jnp.concatenate([l0, l0, l1], axis=0))
        for t in range((here.stop - here.start) // TILE):
            at = slice(t * TILE, (t + 1) * TILE)
            out[:, here.start + t * TILE : here.start + (t + 1) * TILE] = (xc[:, at] - common[:, at]) * scale
        pltpu.make_async_copy(out.at[:, here], out_hbm.at[:, here], out_sem.at[c]).start()
    for c, here in enumerate(bands):
        pltpu.make_async_copy(out.at[:, here], out_hbm.at[:, here], out_sem.at[c]).wait()


def corrected(lines, me, orders, v, x, pixel_total, chunk=512):
    m, n = x.shape
    k = v.shape[0]
    return pl.pallas_call(
        functools.partial(finish_kernel, pixel_total, chunk, orders),
        out_shape=jax.ShapeDtypeStruct((m, n), F32),
        in_specs=[
            pl.BlockSpec(memory_space=pltpu.SMEM),
            pl.BlockSpec(memory_space=pltpu.VMEM),
            pl.BlockSpec(memory_space=pltpu.VMEM),
            pl.BlockSpec(memory_space=pl.ANY),
        ],
        out_specs=pl.BlockSpec(memory_space=pl.ANY),
        scratch_shapes=[
            pltpu.VMEM((m, n), F32),
            pltpu.VMEM((m, n), F32),
            pltpu.VMEM(lines.shape, F32),
            pltpu.VMEM((m, m), BF16),
            pltpu.VMEM((m, m), BF16),
            pltpu.VMEM((m, m), BF16),
            pltpu.VMEM((m, n), BF16),
            pltpu.VMEM((m, n), BF16),
            pltpu.SemaphoreType.DMA,
            pltpu.SemaphoreType.DMA((n // chunk + 1,)),
        ],
        compiler_params=pltpu.CompilerParams(vmem_limit_bytes=VMEM),
        cost_estimate=pl.CostEstimate(flops=12 * m * k * n, bytes_accessed=8 * m * n, transcendentals=0),
        name="finish",
    )(me, lines, v, x)


def on_device(phase_stack, start_basis):
    pixel_total = phase_stack.shape[1] * lax.axis_size(AXES)
    lines, v = sum_everywhere(upper_gram(phase_stack), start_rows(start_basis.T))
    me = jnp.stack([place_on(axis) for axis in SHARED]).astype(jnp.int32)
    orders = tuple(slots_of(axis) for axis in SHARED)
    return corrected(lines, me, orders, v, phase_stack, pixel_total)


def solution(mesh):
    split = Mesh(mesh.devices.reshape(-1, 2, mesh.shape["gy"], mesh.shape["gz"]), AXES)
    placed = (P(None, AXES), P())
    return jax.shard_map(
        on_device, mesh=split, in_specs=placed, out_specs=P(None, AXES), check_vma=False
    )
```
